32 devices in a mesh: dp: 8 (over z, y), tensor: 4 (over x, core).
Axes of the slice: x: 2, y: 2, z: 4, core: 2. Of those that a mesh axis runs over, the one named last changes fastest.
Arguments:
- states: bfloat16 [4096, 2048], P('dp'), may hold values from -6 to 6
- teacher: bfloat16 [4096, 2048], P('dp'), may hold values from -6 to 6
- segments: int32 [4096], P('dp'), may hold values from 0 to 9, as said below
- positions: int32 [4096], P('dp'), may hold values from 0 to 511, as said below
- w_q: bfloat16 [2048, 2048], P('dp', 'tensor'), may hold values from -0.125 to 0.125
- key_matrix: bfloat16 [2048, 1024], P('dp', 'tensor'), may hold values from -0.125 to 0.125
- value_matrix: bfloat16 [2048, 1024], P('dp', 'tensor'), may hold values from -0.125 to 0.125
- w_o: bfloat16 [2048, 2048], P('tensor', 'dp'), may hold values from -0.75 to 0.75
- w_gate: bfloat16 [2048, 8192], P('dp', 'tensor'), may hold values from -0.125 to 0.125
- w_up: bfloat16 [2048, 8192], P('dp', 'tensor'), may hold values from -0.125 to 0.125
- w_down: bfloat16 [8192, 2048], P('tensor', 'dp'), may hold values from -0.0625 to 0.0625
- norm1_gain: bfloat16 [2048], P('dp'), may hold values from 0.5 to 1.5
- norm2_gain: bfloat16 [2048], P('dp'), may hold values from 0.5 to 1.5
Outputs:
- out_states: bfloat16 [4096, 2048], P('dp')
- grad_states: float32 [4096, 2048], P('dp')
- loss_value: float32 [], replicated
- grad_w_q: float32 [2048, 2048], P('dp', 'tensor')
- grad_w_k: float32 [2048, 1024], P('dp', 'tensor')
- grad_w_v: float32 [2048, 1024], P('dp', 'tensor')
- grad_w_o: float32 [2048, 2048], P('tensor', 'dp')
- grad_w_gate: float32 [2048, 8192], P('dp', 'tensor')
- grad_w_up: float32 [2048, 8192], P('dp', 'tensor')
- grad_w_down: float32 [8192, 2048], P('tensor', 'dp')
- grad_norm1_gain: float32 [2048], P('dp')
- grad_norm2_gain: float32 [2048], P('dp')
The draws below stay inside these ranges and needn't reach their ends.
Inputs may be any that keep to these rules, and one draw needn't show every extreme that they name: `segments`: each run of 512 slots is one sequence: documents numbered 1, 2, 3 in order, each of 60 to 512 tokens except that the last may be cut short, then padding numbered 0; the first sequence has no padding and only documents of 60 tokens, its last possibly cut; the last sequence has no padding and a first document of exactly 512 tokens. `positions`: each token's place within its document, counted from 0; 0 on padding.
All inputs are finite; a program needn't handle non-finite values.
Results may differ from the reference program's by a relative error of at most 0.014.
Values may be sent and summed in bfloat16 or wider, within the bound.
No kernel may reach another device: no remote copies, remote signals or barrier semaphores. Data moves between devices by JAX's collectives and lax.ppermute only.
A program may use at most 192 MiB of HBM per device.

```python
import math
import jax
import jax.numpy as jnp
from jax import lax

MODEL_WIDTH = 2048
QUERY_HEADS = 8
KEY_VALUE_HEADS = 4
HEAD_SIZE = 256
FF = 8192
TOK_DEV = 512
DOC_MIN = 60
DOC_MAX = 512
TOKENS = 4096


def layout(key):
    nseqs = TOKENS // TOK_DEV
    ndocs = TOK_DEV // DOC_MIN + 1
    lengths = jax.random.randint(jax.random.fold_in(key, 7), (nseqs, ndocs), DOC_MIN, DOC_MAX + 1)
    row_ids = jnp.arange(nseqs, dtype=jnp.int32)[:, None]
    col_ids = jnp.arange(ndocs, dtype=jnp.int32)[None, :]
    lengths = jnp.where(row_ids == 0, DOC_MIN, lengths)
    lengths = jnp.where((row_ids == nseqs - 1) & (col_ids == 0), DOC_MAX, lengths).astype(jnp.int32)
    ends = jnp.cumsum(lengths, axis=1)
    starts = jnp.concatenate([jnp.zeros((nseqs, 1), jnp.int32), ends[:, :-1]], axis=1)
    slot_ids = jnp.arange(TOK_DEV, dtype=jnp.int32)
    docnum = jnp.sum((slot_ids[None, :, None] >= ends[:, None, :]).astype(jnp.int32), axis=2)
    begins = jnp.take_along_axis(starts, docnum, axis=1)
    seq_ids = jnp.arange(nseqs, dtype=jnp.int32)
    span = jax.random.randint(jax.random.fold_in(key, 5), (), 2 * TOK_DEV // 3, 7 * TOK_DEV // 8 + 1).astype(jnp.int32)
    power = jax.random.randint(jax.random.fold_in(key, 6), (), 1, 4).astype(jnp.int32)
    rest = (nseqs - 1 - seq_ids).astype(jnp.int32)
    rest_two = rest * rest
    rest_three = rest_two * rest
    powered = jnp.where(power == 1, rest, jnp.where(power == 2, rest_two, rest_three))
    top = max(nseqs - 1, 1)
    denom = jnp.where(power == 1, top, jnp.where(power == 2, top * top, top * top * top)).astype(jnp.int32)
    jitter = jax.random.randint(jax.random.fold_in(key, 9), (nseqs,), -(TOK_DEV // 8), TOK_DEV // 8 + 1)
    valid = TOK_DEV - span * powered // denom + jitter.astype(jnp.int32)
    valid = jnp.clip(valid, TOK_DEV // 8, TOK_DEV)
    valid = jnp.where((seq_ids == 0) | (seq_ids == nseqs - 1), TOK_DEV, valid).astype(jnp.int32)
    live_slots = slot_ids[None, :] < valid[:, None]
    seg_ids = jnp.where(live_slots, docnum + 1, 0).astype(jnp.int32)
    places = jnp.where(live_slots, slot_ids[None, :] - begins, 0).astype(jnp.int32)
    return (seg_ids.reshape(TOKENS), places.reshape(TOKENS))


def draw_segments(key, part):
    return layout(jax.random.fold_in(key, 11))[0]


def draw_positions(key, part):
    return layout(jax.random.fold_in(key, 11))[1]


def block_levels(own_key, shape, split, low, high):
    factor_of, own = 1.0, jax.random.fold_in(own_key, 6)
    for position, blocks in split:
        draws = jnp.exp(jax.random.uniform(jax.random.fold_in(own, position), (blocks,), jnp.float32, low / len(split), high / len(split)))
        factor_of = factor_of * jnp.repeat(draws, shape[position] // blocks).reshape([-1 if axis == position else 1 for axis in range(len(shape))])
    return factor_of


def noise(own_key, dims, deviation, reach, cuts=(), kind=jnp.bfloat16):
    loudness = block_levels(own_key, dims, cuts, -0.22, 0.18) if cuts else 1.0
    result = jax.random.normal(own_key, dims, jnp.float32) * deviation * loudness
    return jnp.minimum(jnp.maximum(result, -reach), reach).astype(kind)


def setup_inputs(seed: int = 0) -> dict:
    keys = jax.random.split(jax.random.key(seed), 14)
    states = noise(keys[0], (TOKENS, MODEL_WIDTH), 1.0, 6.0, ((0, 8),))
    teacher = noise(keys[1], (TOKENS, MODEL_WIDTH), 1.0, 6.0, ((0, 8),))
    segments = draw_segments(jax.random.fold_in(keys[13], 71), 0)
    positions = draw_positions(jax.random.fold_in(keys[13], 71), 0)
    w_q = noise(keys[4], (MODEL_WIDTH, QUERY_HEADS * HEAD_SIZE), MODEL_WIDTH ** -0.5, 0.125, ((0, 8), (1, 4)))
    key_matrix = noise(keys[5], (MODEL_WIDTH, KEY_VALUE_HEADS * HEAD_SIZE), MODEL_WIDTH ** -0.5, 0.125, ((0, 8), (1, 4)))
    value_matrix = noise(keys[6], (MODEL_WIDTH, KEY_VALUE_HEADS * HEAD_SIZE), MODEL_WIDTH ** -0.5, 0.125, ((0, 8), (1, 4)))
    w_o = noise(keys[7], (QUERY_HEADS * HEAD_SIZE, MODEL_WIDTH), (QUERY_HEADS * HEAD_SIZE * 16 // DOC_MAX) ** -0.5, 0.75, ((0, 4), (1, 8)))
    w_gate = noise(keys[8], (MODEL_WIDTH, FF), MODEL_WIDTH ** -0.5, 0.125, ((0, 8), (1, 4)))
    w_up = noise(keys[9], (MODEL_WIDTH, FF), MODEL_WIDTH ** -0.5, 0.125, ((0, 8), (1, 4)))
    w_down = noise(keys[10], (FF, MODEL_WIDTH), FF ** -0.5, 0.0625, ((0, 4), (1, 8)))
    norm1_gain = jnp.clip(1.0 + 0.1 * jax.random.normal(keys[11], (MODEL_WIDTH,), jnp.float32), 0.5, 1.5).astype(jnp.bfloat16)
    norm2_gain = jnp.clip(1.0 + 0.1 * jax.random.normal(keys[12], (MODEL_WIDTH,), jnp.float32), 0.5, 1.5).astype(jnp.bfloat16)
    return dict(states=states, teacher=teacher, segments=segments, positions=positions, w_q=w_q, key_matrix=key_matrix, value_matrix=value_matrix, w_o=w_o, w_gate=w_gate, w_up=w_up, w_down=w_down, norm1_gain=norm1_gain, norm2_gain=norm2_gain)


EPS = 1e-06
THETA = 1000042.0
HIGHEST = lax.Precision.HIGHEST

@jax.custom_vjp
def low(v):
    return lax.optimization_barrier(v.astype(jnp.bfloat16)).astype(jnp.float32)

@jax.custom_vjp
def low_back(v):
    return v

def low_keep(v):
    return (low(v), None)

def low_pass(kept, grad):
    return (grad,)

def back_keep(v):
    return (v, None)

def back_low(kept, grad):
    return (low(grad),)
low.defvjp(low_keep, low_pass)
low_back.defvjp(back_keep, back_low)

def tables(places, width):
    halfway = width // 2
    counter = jnp.arange(halfway, dtype=jnp.float32)
    inverse = jnp.exp(counter * (-2.0 * math.log(THETA) / width))
    angles = places.astype(jnp.float32)[..., None] * inverse
    return (jnp.cos(angles), jnp.sin(angles))

def rotate(value_rows, cos_table, sin_table):
    halfway = value_rows.shape[-1] // 2
    first_half = value_rows[..., :halfway]
    second_half = value_rows[..., halfway:]
    return jnp.concatenate([first_half * cos_table - second_half * sin_table, second_half * cos_table + first_half * sin_table], axis=-1)

def rms_scale(value_rows):
    return lax.rsqrt(lax.optimization_barrier(jnp.mean(value_rows * value_rows, axis=-1, keepdims=True)) + EPS)

def forward(params, inputs, teacher_f, seg_ids, places):
    w_q, key_matrix, value_matrix, w_o, w_gate, w_up, w_down, gain_one, gain_two = params
    head_groups = inputs.shape[0]
    sequence_length = inputs.shape[1]
    repeat_factor = QUERY_HEADS // KEY_VALUE_HEADS
    normed = low(inputs * rms_scale(inputs) * gain_one)
    query_rows = low_back(jnp.einsum('gtd,de->gte', normed, w_q, precision=HIGHEST))
    unrotated_keys = low_back(jnp.einsum('gtd,de->gte', normed, key_matrix, precision=HIGHEST))
    value_rows = low(low_back(jnp.einsum('gtd,de->gte', normed, value_matrix, precision=HIGHEST)))
    cos_table, sin_table = tables(places, HEAD_SIZE)
    query_rows = query_rows.reshape(head_groups, sequence_length, KEY_VALUE_HEADS, repeat_factor, HEAD_SIZE).transpose(0, 2, 3, 1, 4)
    unrotated_keys = unrotated_keys.reshape(head_groups, sequence_length, KEY_VALUE_HEADS, HEAD_SIZE).transpose(0, 2, 1, 3)
    value_rows = value_rows.reshape(head_groups, sequence_length, KEY_VALUE_HEADS, HEAD_SIZE).transpose(0, 2, 1, 3)
    rotated_query = low(rotate(query_rows, cos_table[:, None, None], sin_table[:, None, None]))
    rotated_k = low(rotate(unrotated_keys, cos_table[:, None], sin_table[:, None]))
    rows_per_block = min(512, sequence_length)
    block_total = sequence_length // rows_per_block
    query_tiles_list = jnp.moveaxis(rotated_query.reshape(head_groups, KEY_VALUE_HEADS, repeat_factor, block_total, rows_per_block, HEAD_SIZE), 3, 0)
    seg_blocks = jnp.moveaxis(seg_ids.reshape(head_groups, block_total, rows_per_block), 1, 0)
    index_blocks = jnp.arange(sequence_length, dtype=jnp.int32).reshape(block_total, rows_per_block)
    key_index = jnp.arange(sequence_length, dtype=jnp.int32)
    score_scale = 1.0 / math.sqrt(HEAD_SIZE)

    def attend(block_item):
        query_block, seg_query, index_query = block_item
        scores = low_back(score_scale * jnp.einsum('gkrbe,gkte->gkrbt', query_block, rotated_k, precision=HIGHEST))
        allowed = (seg_query[:, None, None, :, None] == seg_ids[:, None, None, None, :]) & (key_index[None, None, None, None, :] <= index_query[None, None, None, :, None])
        scores = jnp.where(allowed, scores, -1e+30)
        largest = lax.optimization_barrier(jnp.max(scores, axis=-1, keepdims=True))
        exponent = jnp.exp(scores - largest)
        weights = exponent / lax.optimization_barrier(jnp.sum(exponent, axis=-1, keepdims=True))
        return jnp.einsum('gkrbt,gkte->gkrbe', low(weights), value_rows, precision=HIGHEST)
    attended_rows = lax.map(jax.checkpoint(attend), (query_tiles_list, seg_blocks, index_blocks))
    attended_rows = jnp.moveaxis(attended_rows, 0, 3).reshape(head_groups, KEY_VALUE_HEADS, repeat_factor, sequence_length, HEAD_SIZE)
    attended_rows = attended_rows.transpose(0, 3, 1, 2, 4).reshape(head_groups, sequence_length, QUERY_HEADS * HEAD_SIZE)
    attended_rows = low(low_back(attended_rows))
    hidden = inputs + low_back(jnp.einsum('gte,ed->gtd', attended_rows, w_o, precision=HIGHEST))
    normed_two = low(hidden * rms_scale(hidden) * gain_two)
    gate_proj = low_back(jnp.einsum('gtd,df->gtf', normed_two, w_gate, precision=HIGHEST))
    up_proj = low_back(jnp.einsum('gtd,df->gtf', normed_two, w_up, precision=HIGHEST))
    active = low(gate_proj * jax.nn.sigmoid(gate_proj) * up_proj)
    output = hidden + low_back(jnp.einsum('gtf,fd->gtd', active, w_down, precision=HIGHEST))
    live_mask = (seg_ids > 0).astype(inputs.dtype)
    squares = jnp.sum(live_mask[..., None] * (output - teacher_f) ** 2)
    return (output, squares)

def reference(states, teacher, segments, positions, w_q, key_matrix, value_matrix, w_o, w_gate, w_up, w_down, norm1_gain, norm2_gain):
    params = tuple((item.astype(jnp.float32) for item in (w_q, key_matrix, value_matrix, w_o, w_gate, w_up, w_down, norm1_gain, norm2_gain)))
    nseqs = TOKENS // TOK_DEV
    group_size = 1
    for candidate in range(1, nseqs + 1):
        if nseqs % candidate == 0 and candidate * TOK_DEV <= 4096:
            group_size = candidate
    step_count = nseqs // group_size
    count = jnp.sum((segments > 0).astype(jnp.float32))
    loss_weight = TOKENS / (2.0 * count)

    def regroup(array):
        return array.reshape((step_count, group_size, TOK_DEV) + array.shape[1:])
    inputs_all = regroup(states.astype(jnp.float32))
    teacher_all = regroup(teacher.astype(jnp.float32))
    seg_all = regroup(segments)
    place_all = regroup(positions)

    def one_group(carry, group_item):
        inputs_g, teacher_g, seg_g, place_g = group_item

        def run(params_in, inputs_in):
            return forward(params_in, inputs_in, teacher_g, seg_g, place_g)
        (output_g, squares_g), pullback = jax.vjp(run, params, inputs_g)
        grad_params, grad_inputs = pullback((jnp.zeros_like(output_g), loss_weight))
        grads_sum, squares_sum = carry
        grads_sum = jax.tree.map(jnp.add, grads_sum, grad_params)
        return ((grads_sum, squares_sum + squares_g), (output_g, grad_inputs))
    init = (tuple((jnp.zeros_like(item) for item in params)), jnp.zeros((), jnp.float32))
    (grads, squares_total), (outputs, grad_inputs) = lax.scan(one_group, init, (inputs_all, teacher_all, seg_all, place_all))
    loss_value = squares_total / (count * MODEL_WIDTH)
    out_states = outputs.reshape(TOKENS, MODEL_WIDTH).astype(jnp.bfloat16)
    grad_states = grad_inputs.reshape(TOKENS, MODEL_WIDTH)
    return (out_states, grad_states, loss_value, grads[0], grads[1], grads[2], grads[3], grads[4], grads[5], grads[6], grads[7], grads[8])
```

```python
import math

import jax
import jax.numpy as jnp
from jax import lax
from jax.sharding import PartitionSpec as P

MODEL_WIDTH = 2048
HEAD_SIZE = 256

EPS = 1e-06
THETA = 1000042.0
AXES = ("dp", "tensor")
BF = jnp.bfloat16
F32 = jnp.float32


class Net:
    def __init__(self):
        self.dp = lax.axis_size("dp")
        self.tensor = lax.axis_size("tensor")
        self.ring = self.dp // 2
        d = lax.axis_index("dp")
        t = lax.axis_index("tensor")
        self.z, self.y = d // 2, d % 2
        self.x, self.c = t // 2, t % 2

    def _perm(self, move):
        pairs = []
        for z in range(self.ring):
            for y in range(2):
                for x in range(2):
                    for c in range(2):
                        tz, ty, tx, tc = move(z, y, x, c)
                        pairs.append(
                            (
                                (z * 2 + y) * self.tensor + x * 2 + c,
                                ((tz % self.ring) * 2 + ty) * self.tensor + tx * 2 + tc,
                            )
                        )
        return pairs

    def flip_x(self, v):
        return lax.ppermute(v, AXES, self._perm(lambda z, y, x, c: (z, y, 1 - x, c)))

    def flip_y(self, v):
        return lax.ppermute(v, AXES, self._perm(lambda z, y, x, c: (z, 1 - y, x, c)))

    def flip_c(self, v):
        return lax.ppermute(v, AXES, self._perm(lambda z, y, x, c: (z, y, x, 1 - c)))

    def shift(self, v, by):
        return lax.ppermute(v, AXES, self._perm(lambda z, y, x, c: (z + by, y, x, c)))

    def swap_z(self, v, bit):
        return lax.ppermute(v, AXES, self._perm(lambda z, y, x, c: (z ^ bit, y, x, c)))

    def all_sum(self, v):
        v = v + self.flip_c(v)
        v = v + self.flip_x(v)
        return self.dp_sum(v)

    def dp_sum(self, v):
        v = v + self.flip_y(v)
        bit = 1
        while bit < self.ring:
            v = v + self.swap_z(v, bit)
            bit *= 2
        return v

    def ring_gather(self, v):
        ring, half = self.ring, v.shape[0] // 2
        pieces = [v] + [None] * (ring - 1)
        fwd = bwd = v
        for step in range(1, ring // 2):
            fwd = self.shift(fwd, 1)
            bwd = self.shift(bwd, -1)
            pieces[ring - step], pieces[step] = fwd, bwd
        lo = self.shift(fwd[:half], 1)
        hi = self.shift(bwd[half:], -1)
        pieces[ring // 2] = jnp.concatenate([lo, hi], axis=0)
        return pieces

    def ring_reduce(self, pieces):
        ring, half = self.ring, pieces[0].shape[0] // 2
        far = ring // 2
        fwd = self.shift(pieces[far][:half].astype(BF), 1)
        bwd = self.shift(pieces[far][half:].astype(BF), -1)
        for step in range(far - 1, 0, -1):
            up, down = pieces[step].astype(F32), pieces[ring - step].astype(F32)
            if step == far - 1:
                up = jnp.concatenate([up[:half] + fwd.astype(F32), up[half:]], axis=0)
                down = jnp.concatenate([down[:half], down[half:] + bwd.astype(F32)], axis=0)
            else:
                up = up + fwd.astype(F32)
                down = down + bwd.astype(F32)
            fwd = self.shift(up.astype(BF), 1)
            bwd = self.shift(down.astype(BF), -1)
        return pieces[0].astype(F32) + fwd.astype(F32) + bwd.astype(F32)

    def ring_gather_small(self, v):
        return [v] + [self.shift(v, -k) for k in range(1, self.ring)]

    def ring_reduce_small(self, pieces):
        total = pieces[0]
        for k in range(1, self.ring):
            total = total + self.shift(pieces[k], k)
        return total

    def y_order(self, mine, other, axis):
        first = jnp.where(self.y == 0, mine, other)
        second = jnp.where(self.y == 0, other, mine)
        return jnp.concatenate([first, second], axis=axis)

    def split_y(self, v, axis):
        n = v.shape[axis] // 2
        mine = lax.dynamic_slice_in_dim(v, self.y * n, n, axis)
        other = lax.dynamic_slice_in_dim(v, (1 - self.y) * n, n, axis)
        return mine, other

    def plane_gather(self, v):
        half = v.shape[0] // 2
        a = self.flip_x(v)
        b = self.flip_y(v)
        lo = self.flip_y(a[:half])
        hi = self.flip_x(b[half:])
        mine = jnp.concatenate([v, a, b, lo, hi], axis=0)
        other = self.flip_c(mine)
        return jnp.concatenate([mine, other], axis=0)

    def plane_reduce(self, v):
        rows = v.shape[0] // 2
        n = rows // 4
        half = n // 2
        got = self.flip_c(v[rows:].astype(BF))
        s = v[:rows] + got.astype(F32)
        own, a, b, dg = s[:n], s[n : 2 * n], s[2 * n : 3 * n], s[3 * n :]
        r1 = self.flip_x(dg[:half].astype(BF)).astype(F32)
        r2 = self.flip_y(dg[half:].astype(BF)).astype(F32)
        b = jnp.concatenate([b[:half] + r1, b[half:]], axis=0)
        a = jnp.concatenate([a[:half], a[half:] + r2], axis=0)
        ra = self.flip_x(a.astype(BF))
        rb = self.flip_y(b.astype(BF))
        return own + ra.astype(F32) + rb.astype(F32)


def after(value, *deps):
    return lax.optimization_barrier((value,) + deps)[0]


def tables(places, width):
    halfway = width // 2
    counter = jnp.arange(halfway, dtype=jnp.float32)
    inverse = jnp.exp(counter * (-2.0 * math.log(THETA) / width))
    angles = places.astype(jnp.float32)[..., None] * inverse
    return (jnp.cos(angles), jnp.sin(angles))


def rotate(value_rows, cos_table, sin_table):
    halfway = value_rows.shape[-1] // 2
    first_half = value_rows[..., :halfway]
    second_half = value_rows[..., halfway:]
    return jnp.concatenate(
        [
            first_half * cos_table - second_half * sin_table,
            second_half * cos_table + first_half * sin_table,
        ],
        axis=-1,
    )


def unrotate(grads_in, cos_table, sin_table):
    return rotate(grads_in, cos_table, -sin_table)


def rms_scale(value_rows):
    return lax.rsqrt(jnp.mean(value_rows * value_rows, axis=-1, keepdims=True) + EPS)


def norm_back(grad_normed, unit_rows, recip_rows, gain_full):
    scaled = grad_normed * gain_full
    gain_grad = jnp.sum(grad_normed * unit_rows, axis=0)
    grad_rows = recip_rows * (
        scaled - unit_rows * jnp.mean(scaled * unit_rows, axis=-1, keepdims=True)
    )
    return (gain_grad, grad_rows)


def dot(left, right):
    return jnp.dot(left, right, preferred_element_type=F32)


def token_dot(left, right):
    return lax.dot_general(
        left, right, (((0,), (0,)), ((), ())), preferred_element_type=jnp.float32
    )


def dot_trans(left, right):
    return lax.dot_general(
        left, right, (((1,), (1,)), ((), ())), preferred_element_type=jnp.float32
    )


def per_device(
    states,
    teacher,
    segments,
    positions,
    w_q,
    key_matrix,
    value_matrix,
    w_o,
    w_gate,
    w_up,
    w_down,
    norm1_gain,
    norm2_gain,
):
    net = Net()
    ring = net.ring
    seq, width = states.shape
    rp = w_q.shape[0]
    rows2 = 2 * rp
    tok = seq // 4
    fq, fk = w_q.shape[1], key_matrix.shape[1]
    heads_kv = fk // HEAD_SIZE
    rep = fq // fk
    hid = w_gate.shape[1] // 2

    def roll(v, back=False):
        start = net.z * rows2
        start = (width - start) if back else start
        twice = jnp.concatenate([v, v], axis=-1)
        return lax.dynamic_slice_in_dim(twice, start, width, axis=v.ndim - 1)

    gains = jnp.stack([norm1_gain, norm2_gain])
    gains = net.y_order(gains, net.flip_y(gains), axis=1)
    gains = jnp.concatenate(net.ring_gather_small(gains), axis=1).astype(F32)
    gain_one, gain_two = gains[0:1], gains[1:2]
    live = (segments > 0).astype(F32)
    count = net.dp_sum(jnp.full((8, 128), jnp.sum(live), F32))[0, 0]

    q2 = net.y_order(w_q, net.flip_y(w_q), axis=0)
    full_q = jnp.concatenate(net.ring_gather(q2), axis=0)
    kv = jnp.concatenate([key_matrix, value_matrix], axis=1)
    kv_mine = jnp.stack(net.ring_gather(kv))
    full_kv = net.y_order(kv_mine, net.flip_y(kv_mine), axis=1).reshape(width, 2 * fk)
    w_o, w_gate, w_up = after((w_o, w_gate, w_up), kv_mine, full_q)
    o_mine = jnp.stack(net.ring_gather(w_o), axis=1)
    o_other = net.flip_y(o_mine)
    full_o = jnp.stack(
        [jnp.where(net.y == 0, o_mine, o_other), jnp.where(net.y == 0, o_other, o_mine)], axis=2
    ).reshape(w_o.shape[0], width)

    def fetch_in(w):
        mine, other = net.split_y(w, 1)
        shard = net.y_order(mine, net.flip_y(other), axis=0)
        return jnp.concatenate(net.ring_gather(shard), axis=0)

    full_gate = fetch_in(w_gate)
    full_up = fetch_in(w_up)
    w_down = after(w_down, full_up)
    mine, other = net.split_y(w_down, 0)
    shard = net.y_order(mine, net.flip_y(other), axis=1)
    full_down = jnp.concatenate(net.ring_gather(shard), axis=1)

    inputs = roll(states).astype(F32)
    recip_one = rms_scale(inputs)
    unit_one = inputs * recip_one
    normed = (unit_one * gain_one).astype(BF)
    query_rows = dot(normed, full_q).reshape(seq, heads_kv, rep, HEAD_SIZE).transpose(1, 2, 0, 3)
    kv_rows = dot(normed, full_kv)
    keys = kv_rows[:, :fk].reshape(seq, heads_kv, HEAD_SIZE).transpose(1, 0, 2)
    value_rows = kv_rows[:, fk:].astype(BF).reshape(seq, heads_kv, HEAD_SIZE).transpose(1, 0, 2)
    cos_table, sin_table = tables(positions, HEAD_SIZE)
    rotated_query = rotate(query_rows, cos_table, sin_table).astype(BF)
    rotated_k = rotate(keys, cos_table, sin_table).astype(BF)
    score_scale = 1.0 / math.sqrt(HEAD_SIZE)
    key_index = jnp.arange(seq, dtype=jnp.int32)
    scores = (
        jnp.einsum("krbe,kte->krbt", rotated_query, rotated_k, preferred_element_type=F32)
        * score_scale
    )
    allowed = (segments[:, None] == segments[None, :]) & (key_index[None, :] <= key_index[:, None])
    scores = jnp.where(allowed, scores, -1e30)
    largest = jnp.max(scores, axis=-1, keepdims=True)
    exponent = jnp.exp(scores - largest)
    weights = exponent / jnp.sum(exponent, axis=-1, keepdims=True)
    weights_low = weights.astype(BF)
    attended = jnp.einsum("krbt,kte->krbe", weights_low, value_rows, preferred_element_type=F32)
    attended = attended.transpose(2, 0, 1, 3).reshape(seq, fq).astype(BF)
    partial = dot(attended, full_o).reshape(2, 2, tok, width)

    keep = lax.dynamic_index_in_dim(partial, net.c, 1, keepdims=False)
    send = lax.dynamic_index_in_dim(partial, 1 - net.c, 1, keepdims=False)
    partial = keep + net.flip_c(send.astype(BF)).astype(F32)
    keep = lax.dynamic_index_in_dim(partial, net.x, 0, keepdims=False)
    send = lax.dynamic_index_in_dim(partial, 1 - net.x, 0, keepdims=False)
    attn_sum = keep + net.flip_x(send.astype(BF)).astype(F32)

    first_token = (net.x * 2 + net.c) * tok
    my_inputs = roll(lax.dynamic_slice_in_dim(states, first_token, tok, 0)).astype(F32)
    my_teacher = roll(lax.dynamic_slice_in_dim(teacher, first_token, tok, 0)).astype(F32)
    my_live = lax.dynamic_slice_in_dim(live, first_token, tok, 0)

    hidden = my_inputs + attn_sum
    recip_two = rms_scale(hidden)
    unit_two = hidden * recip_two
    normed_two = net.plane_gather((unit_two * gain_two).astype(BF))
    gate_proj = dot(normed_two, full_gate)
    up_proj = dot(normed_two, full_up)
    sigmoid_gate = jax.nn.sigmoid(gate_proj)
    silu_gate = gate_proj * sigmoid_gate
    active = (silu_gate * up_proj).astype(BF)
    mlp_sum = net.plane_reduce(dot(active, full_down))
    output = hidden + mlp_sum
    error = (output - my_teacher) * my_live[:, None]
    factor = net.dp * seq / count
    grad_out = error * factor
    squares = jnp.sum(error * error)

    def share_tokens(v):
        def order(flag, mine, other, axis):
            return jnp.concatenate(
                [jnp.where(flag == 0, mine, other), jnp.where(flag == 0, other, mine)], axis=axis
            )

        v = order(net.x, v, net.flip_x(v), 0).reshape(2, tok, width)
        v = jnp.stack([v, net.flip_c(v)])
        v = jnp.where(net.c == 0, v, v[::-1])
        return v.transpose(1, 0, 2, 3).reshape(seq, width)

    out_states = roll(share_tokens(output.astype(BF)), back=True)

    grad_out_low = net.plane_gather(grad_out.astype(BF))
    grad_wdown = token_dot(active, grad_out_low)
    grad_active = dot_trans(grad_out_low, full_down)
    grad_gate = (
        grad_active * up_proj * sigmoid_gate * (1.0 + gate_proj * (1.0 - sigmoid_gate))
    ).astype(BF)
    grad_up = (grad_active * silu_gate).astype(BF)
    grad_wgate = token_dot(normed_two, grad_gate)
    grad_wup = token_dot(normed_two, grad_up)
    back_two = net.plane_reduce(dot_trans(grad_gate, full_gate) + dot_trans(grad_up, full_up))
    gain_two_grad, hidden_from_norm = norm_back(back_two, unit_two, recip_two, gain_two)
    grad_hidden = grad_out + hidden_from_norm
    grad_hidden_low = share_tokens(grad_hidden.astype(BF))

    grad_wo = token_dot(attended, grad_hidden_low)
    grad_attended = dot_trans(grad_hidden_low, full_o).astype(BF)
    grad_attended = grad_attended.reshape(seq, heads_kv, rep, HEAD_SIZE).transpose(1, 2, 0, 3)
    grad_weights = jnp.einsum(
        "krbe,kte->krbt", grad_attended, value_rows, preferred_element_type=F32
    )
    inner = jnp.sum(weights * grad_weights, axis=-1, keepdims=True)
    grad_scores = (weights * (grad_weights - inner)).astype(BF)
    grad_q = (
        jnp.einsum("krbt,kte->krbe", grad_scores, rotated_k, preferred_element_type=F32)
        * score_scale
    )
    grad_k = (
        jnp.einsum("krbt,krbe->kte", grad_scores, rotated_query, preferred_element_type=F32)
        * score_scale
    )
    grad_v = jnp.einsum("krbt,krbe->kte", weights_low, grad_attended, preferred_element_type=F32)
    grad_q = unrotate(grad_q, cos_table, sin_table).astype(BF)
    grad_q = grad_q.transpose(2, 0, 1, 3).reshape(seq, fq)
    grad_k = unrotate(grad_k, cos_table, sin_table).astype(BF)
    grad_k = grad_k.transpose(1, 0, 2).reshape(seq, fk)
    grad_v = grad_v.astype(BF).transpose(1, 0, 2).reshape(seq, fk)
    grad_kv = jnp.concatenate([grad_k, grad_v], axis=1)
    grad_wq = token_dot(normed, grad_q)
    grad_wkv = token_dot(normed, grad_kv)
    back_one = (dot_trans(grad_q, full_q) + dot_trans(grad_kv, full_kv)).reshape(2, 2, tok, width)
    keep = lax.dynamic_index_in_dim(back_one, net.c, 1, keepdims=False)
    send = lax.dynamic_index_in_dim(back_one, 1 - net.c, 1, keepdims=False)
    back_one = (keep + net.flip_c(send.astype(BF)).astype(F32)).astype(BF)
    back_one = back_one.astype(F32) + net.flip_x(back_one).astype(F32)

    def of_core(v):
        v = v.reshape((2, 2, tok) + v.shape[1:])
        return lax.dynamic_index_in_dim(v, net.c, 1, keepdims=False)

    unit_mine, recip_mine = of_core(unit_one), of_core(recip_one)
    scaled = back_one * gain_one
    gain_one_grad = jnp.sum(back_one * unit_mine, axis=(0, 1))
    grad_input = of_core(grad_hidden_low).astype(F32) + recip_mine * (
        scaled - unit_mine * jnp.mean(scaled * unit_mine, axis=-1, keepdims=True)
    )
    grad_input = jnp.stack([grad_input, net.flip_c(grad_input)])
    grad_input = jnp.where(net.c == 0, grad_input, grad_input[::-1])
    grad_input = roll(grad_input.transpose(1, 0, 2, 3).reshape(seq, width), back=True)

    def blocks(v, axis):
        n = v.shape[axis] // ring
        return [lax.slice_in_dim(v, k * n, (k + 1) * n, axis=axis) for k in range(ring)]

    def send_in(g):
        part = net.ring_reduce(blocks(g, 0))
        mine, other = net.split_y(part, 0)
        return net.y_order(mine, net.flip_y(other.astype(BF)).astype(F32), axis=1)

    part = net.ring_reduce(blocks(grad_wdown, 1))
    mine, other = net.split_y(part, 1)
    result_down = net.y_order(mine, net.flip_y(other.astype(BF)).astype(F32), axis=0)
    result_gate = send_in(grad_wgate)
    result_up = send_in(grad_wup)

    part = net.ring_reduce(blocks(grad_wo, 1))
    mine, other = net.split_y(part, 1)
    result_o = mine + net.flip_y(other.astype(BF)).astype(F32)

    part = net.ring_reduce(blocks(grad_wq, 0))
    mine, other = net.split_y(part, 0)
    result_q = mine + net.flip_y(other.astype(BF)).astype(F32)

    mine, other = net.split_y(grad_wkv.reshape(ring, 2, rp, 2 * fk), 1)
    part = mine + net.flip_y(other.astype(BF)).astype(F32)
    result_kv = net.ring_reduce([part[k, 0] for k in range(ring)])
    result_k, result_v = result_kv[:, :fk], result_kv[:, fk:]

    def gain_sum(v, both_x):
        v = v.reshape(ring, 2, rp)
        v = v + net.flip_c(v)
        if both_x:
            v = v + net.flip_x(v)
        mine, other = net.split_y(v, 1)
        v = (mine + net.flip_y(other))[:, 0]
        return net.ring_reduce_small([v[k] for k in range(ring)])

    result_g2 = gain_sum(gain_two_grad, True)
    result_g1 = gain_sum(gain_one_grad, False)
    squares_sum = net.all_sum(jnp.full((8, 128), squares, F32))[0, 0]
    loss_value = squares_sum / (count * width)
    return (
        out_states,
        grad_input,
        loss_value,
        result_q,
        result_k,
        result_v,
        result_o,
        result_gate,
        result_up,
        result_down,
        result_g1,
        result_g2,
    )


def solution(mesh):
    in_specs = (
        P("dp", None),
        P("dp", None),
        P("dp"),
        P("dp"),
        P("dp", "tensor"),
        P("dp", "tensor"),
        P("dp", "tensor"),
        P("tensor", "dp"),
        P("dp", "tensor"),
        P("dp", "tensor"),
        P("tensor", "dp"),
        P("dp"),
        P("dp"),
    )
    out_specs = (
        P("dp", None),
        P("dp", None),
        P(),
        P("dp", "tensor"),
        P("dp", "tensor"),
        P("dp", "tensor"),
        P("tensor", "dp"),
        P("dp", "tensor"),
        P("dp", "tensor"),
        P("tensor", "dp"),
        P("dp"),
        P("dp"),
    )
    return jax.shard_map(
        per_device, mesh=mesh, in_specs=in_specs, out_specs=out_specs, check_vma=False
    )
```

```python
import functools
import math

import jax
import jax.numpy as jnp
from jax import lax
from jax.experimental import pallas as pl
from jax.experimental.pallas import tpu as pltpu
from jax.sharding import PartitionSpec as P

HEAD_SIZE = 256

EPS = 1e-06
THETA = 1000042.0
AXES = ("dp", "tensor")
BF = jnp.bfloat16
F32 = jnp.float32
EXTRA = 16
LIMIT = 56 * 1024 * 1024


class Net:
    def __init__(self):
        self.dp = lax.axis_size("dp")
        self.tensor = lax.axis_size("tensor")
        self.bits = self.dp.bit_length() - 1
        self.far = self.dp // 4
        self.d = lax.axis_index("dp")
        t = lax.axis_index("tensor")
        self.y, self.l, self.f = self.d % 2, (self.d // 2) % 2, self.d // 4
        self.x, self.c = t // 2, t % 2
        self.far_groups = [[4 * f + low for f in range(self.far)] for low in range(4)]

    def flip(self, v, dp_mask, tensor_mask=0):
        pairs = []
        for d in range(self.dp):
            for t in range(self.tensor):
                there = (d ^ dp_mask) * self.tensor + (t ^ tensor_mask)
                pairs.append((d * self.tensor + t, there))
        return lax.ppermute(v, AXES, pairs)

    def flip_y(self, v):
        return self.flip(v, 1)

    def flip_l(self, v):
        return self.flip(v, 2)

    def flip_x(self, v):
        return self.flip(v, 0, 2)

    def flip_c(self, v):
        return self.flip(v, 0, 1)

    def dp_sum(self, v):
        for bit in range(self.bits):
            v = v + self.flip(v, 1 << bit)
        return v

    def far_gather(self, v):
        pieces = [v]
        bit = 4
        while bit < self.dp:
            sent = pieces[0] if len(pieces) == 1 else jnp.stack(pieces)
            got = self.flip(sent, bit)
            pieces = pieces + ([got] if len(pieces) == 1 else [got[k] for k in range(len(pieces))])
            bit *= 2
        return pieces

    def absolute(self, pieces, axis):
        if self.far == 2:
            return in_order(self.f, *pieces, axis)
        stack = jnp.stack(pieces)
        return jnp.concatenate(
            [
                lax.dynamic_index_in_dim(stack, jnp.bitwise_xor(self.f, n), 0, keepdims=False)
                for n in range(self.far)
            ],
            axis=axis,
        )

    def far_reduce(self, pieces, *deps):
        bit = self.dp // 2
        while bit >= 4:
            n = len(pieces) // 2
            sent = pieces[n:]
            got = self.flip(sent[0] if n == 1 else jnp.stack(sent), bit)
            got = after(got, *deps) if deps else got
            got = [got] if n == 1 else [got[k] for k in range(n)]
            pieces = [
                p.astype(F32) + g.astype(F32) if n == 1 else (p.astype(F32) + g.astype(F32)).astype(BF)
                for p, g in zip(pieces[:n], got)
            ]
            bit //= 2
        return pieces[0]

    def cube_gather(self, v):
        parts = [v[a:b] for a, b in part_rows(v.shape[0])]
        for step in range(2):
            got = [self.cube_flip(n, step, part) for n, part in enumerate(parts)]
            parts = [jnp.concatenate(pair, axis=0) for pair in zip(parts, got)]
        last = [self.cube_flip(n, 2, part) for n, part in enumerate(parts)]
        return parts, last

    def cube_flip(self, part, step, v):
        return (self.flip_l, self.flip_y, self.flip_x)[(part + step) % 3](v)

    def cube_reduce(self, near, last):
        got = [self.cube_flip(n, 2, v.astype(BF)) for n, v in enumerate(last)]
        parts = [a.astype(F32) + b.astype(F32) for a, b in zip(near, got)]
        for step in (1, 0):
            half = [v.shape[0] // 2 for v in parts]
            got = [
                self.cube_flip(n, step, v[h:].astype(BF)) for n, (v, h) in enumerate(zip(parts, half))
            ]
            parts = [v[:h] + g.astype(F32) for v, h, g in zip(parts, half, got)]
        return jnp.concatenate(parts, axis=0)


def part_rows(n):
    one = -(-n // 48) * 16
    return [(0, one), (one, 2 * one), (2 * one, n)]


def split_parts(v, n):
    out, at = [], 0
    for a, b in part_rows(n):
        out.append(v[at : at + 4 * (b - a)])
        at += 4 * (b - a)
    return out


def in_order(flag, mine, other, axis):
    first = jnp.where(flag == 0, mine, other)
    second = jnp.where(flag == 0, other, mine)
    return jnp.concatenate([first, second], axis=axis)


def halves(flag, v, axis):
    n = v.shape[axis] // 2
    mine = lax.dynamic_slice_in_dim(v, flag * n, n, axis)
    other = lax.dynamic_slice_in_dim(v, (1 - flag) * n, n, axis)
    return mine, other


def after(value, *deps):
    return lax.optimization_barrier((value,) + deps)[0]


def pin(*values):
    return lax.optimization_barrier(values)


def nt(left, right):
    return lax.dot_general(left, right, (((1,), (1,)), ((), ())), preferred_element_type=F32)


def tn(left, right):
    return lax.dot_general(left, right, (((0,), (0,)), ((), ())), preferred_element_type=F32)


def dot(left, right):
    return jnp.dot(left, right, preferred_element_type=F32)


def spin(v, cos, sin):
    half = v.shape[-1] // 2
    a, b = v[:, :half], v[:, half:]
    return jnp.concatenate([a * cos - b * sin, b * cos + a * sin], axis=-1)


def attend_kernel(far, *refs):
    me, states, cos_ref, sin_ref, seg_col, seg_row, *weights = refs[:10]
    n1_ref, qr_ref, kr_ref, v_ref, p_ref, o_ref = refs[10:]
    seq, width = states.shape
    rp = width // (4 * far)
    fq, fk = qr_ref.shape[1], kr_ref.shape[1]
    tile = min(128, seq)
    scale = 1.0 / math.sqrt(HEAD_SIZE)
    d = me[0]

    @pl.loop(0, seq // tile)
    def _(number):
        rows = pl.ds(pl.multiple_of(number * tile, tile), tile)
        xf = states[rows, :].astype(F32)
        recip = lax.rsqrt(jnp.mean(xf * xf, axis=-1, keepdims=True) + EPS)
        total = None
        for j in range(2):
            for i in range(2):
                for k in range(far):
                    at = jnp.bitwise_xor(d, 4 * k + 2 * i + j)
                    if rp % 128 == 0:
                        block = states[rows, pl.ds(pl.multiple_of(at * rp, 128), rp)].astype(F32)
                    else:
                        first = pl.multiple_of((at // 2) * (2 * rp), 128)
                        block = states[rows, pl.ds(first, 2 * rp)].astype(F32)
                        block = jnp.where(at % 2 == 0, block[:, :rp], block[:, rp:])
                    w = weights[2 * j + i]
                    gain = w[k, rp : rp + EXTRA, :rp][:1].astype(F32)
                    normed = (block * recip * gain).astype(BF)
                    place = ((j * 2 + i) * far + k) * rp
                    n1_ref[rows, place : place + rp] = normed
                    part = dot(normed, w[k, :rp, :])
                    total = part if total is None else total + part
        cos, sin = cos_ref[rows, :], sin_ref[rows, :]
        for head in range(fq // HEAD_SIZE):
            block = slice(head * HEAD_SIZE, (head + 1) * HEAD_SIZE)
            qr_ref[rows, block] = spin(total[:, block], cos, sin).astype(BF)
        for head in range(fk // HEAD_SIZE):
            block = slice(head * HEAD_SIZE, (head + 1) * HEAD_SIZE)
            at = fq + head * HEAD_SIZE
            kr_ref[rows, block] = spin(total[:, at : at + HEAD_SIZE], cos, sin).astype(BF)
        v_ref[rows, :] = total[:, fq + fk :].astype(BF)

    rep = fq // fk
    for i in range(seq // tile):
        rows, keys = slice(i * tile, (i + 1) * tile), slice(0, (i + 1) * tile)
        shape = (tile, (i + 1) * tile)
        behind = lax.broadcasted_iota(jnp.int32, shape, 1) <= (
            lax.broadcasted_iota(jnp.int32, shape, 0) + i * tile
        )
        allowed = (seg_col[rows, :] == seg_row[:, keys]) & behind
        for head in range(fq // HEAD_SIZE):
            block = slice(head * HEAD_SIZE, (head + 1) * HEAD_SIZE)
            k = head // rep
            kblock = slice(k * HEAD_SIZE, (k + 1) * HEAD_SIZE)
            s = nt(qr_ref[rows, block], kr_ref[keys, kblock]) * scale
            s = jnp.where(allowed, s, -1e30)
            e = jnp.exp(s - jnp.max(s, axis=-1, keepdims=True))
            p = (e / jnp.sum(e, axis=-1, keepdims=True)).astype(BF)
            p_ref[head, rows, keys] = p
            o_ref[rows, block] = dot(p, v_ref[keys, kblock]).astype(BF)


def attend(me, states, cos, sin, segments, weights, fq, fk, far):
    seq, width = states.shape
    shapes = [
        jax.ShapeDtypeStruct((seq, width), BF),
        jax.ShapeDtypeStruct((seq, fq), BF),
        jax.ShapeDtypeStruct((seq, fk), BF),
        jax.ShapeDtypeStruct((seq, fk), BF),
        jax.ShapeDtypeStruct((fq // HEAD_SIZE, seq, seq), BF),
        jax.ShapeDtypeStruct((seq, fq), BF),
    ]
    vmem = pl.BlockSpec(memory_space=pltpu.VMEM)
    flops = 2 * seq * width * (fq + 2 * fk) + 4 * seq * seq * fq
    return pl.pallas_call(
        functools.partial(attend_kernel, far),
        out_shape=shapes,
        in_specs=[pl.BlockSpec(memory_space=pltpu.SMEM)] + [vmem] * 9,
        out_specs=[vmem] * 6,
        compiler_params=pltpu.CompilerParams(vmem_limit_bytes=LIMIT),
        cost_estimate=pl.CostEstimate(
            flops=flops, bytes_accessed=12 << 20, transcendentals=seq * seq * 2
        ),
        name="attend",
    )(me, states, cos, sin, segments[:, None], segments[None, :], *weights)


def attend_back_kernel(far, *refs):
    me, dh, w_o, qr_ref, kr_ref, v_ref, p_ref, cos_ref, sin_ref, *weights = refs[:13]
    d_ref, send_ref, keep_ref = refs[13:16]
    do_ref, dk_ref, dv_ref = refs[16:]
    seq, width = dh.shape
    rp = width // (4 * far)
    fq, fk = qr_ref.shape[1], kr_ref.shape[1]
    tile = min(128, seq)
    scale = 1.0 / math.sqrt(HEAD_SIZE)
    rep = fq // fk

    @pl.loop(0, seq // tile)
    def _(i):
        rows = pl.ds(pl.multiple_of(i * tile, tile), tile)
        do_ref[rows, :] = nt(dh[rows, :], w_o[...]).astype(BF)

    dk_ref[...] = jnp.zeros_like(dk_ref)
    dv_ref[...] = jnp.zeros_like(dv_ref)
    for i in range(seq // tile):
        rows, keys = slice(i * tile, (i + 1) * tile), slice(0, (i + 1) * tile)
        cos, sin = cos_ref[rows, :], -sin_ref[rows, :]
        for head in range(fq // HEAD_SIZE):
            block = slice(head * HEAD_SIZE, (head + 1) * HEAD_SIZE)
            k = head // rep
            kblock = slice(k * HEAD_SIZE, (k + 1) * HEAD_SIZE)
            do = do_ref[rows, block]
            pb = p_ref[head, rows, keys]
            p = pb.astype(F32)
            dp = nt(do, v_ref[keys, kblock])
            inner = jnp.sum(p * dp, axis=-1, keepdims=True)
            ds = (p * (dp - inner)).astype(BF)
            dq = dot(ds, kr_ref[keys, kblock]) * scale
            d_ref[rows, block] = spin(dq, cos, sin).astype(BF)
            dk_ref[keys, kblock] += tn(ds, qr_ref[rows, block])
            dv_ref[keys, kblock] += tn(pb, do)
    for head in range(fk // HEAD_SIZE):
        block = slice(head * HEAD_SIZE, (head + 1) * HEAD_SIZE)
        at = fq + head * HEAD_SIZE
        d_ref[:, at : at + HEAD_SIZE] = spin(
            dk_ref[:, block] * scale, cos_ref[...], -sin_ref[...]
        ).astype(BF)
    d_ref[:, fq + fk :] = dv_ref[...].astype(BF)

    tok = seq // 4
    mine, d = me[1], me[0]
    for side in range(2):
        out = slice(side * tok, (side + 1) * tok)
        for ref, which in ((send_ref, 1 - mine), (keep_ref, mine)):
            rows = pl.ds(pl.multiple_of((side * 2 + which) * tok, tok), tok)
            grad = d_ref[rows, :]
            for i in range(2):
                for k in range(far):
                    values = [
                        nt(grad, weights[2 * j + i][k, :rp, :]).astype(BF) for j in range(2)
                    ]
                    at = jnp.bitwise_xor(d, 4 * k + 2 * i)
                    if rp % 128 == 0:
                        for j in range(2):
                            place = pl.multiple_of(jnp.bitwise_xor(at, j) * rp, 128)
                            ref[out, pl.ds(place, rp)] = values[j]
                    else:
                        place = pl.multiple_of((at // 2) * (2 * rp), 128)
                        pair = [jnp.concatenate(v, axis=-1) for v in (values, values[::-1])]
                        ref[out, pl.ds(place, 2 * rp)] = jnp.where(at % 2 == 0, *pair)


def attend_back(me, dh, w_o, qr, kr, v, p, cos, sin, weights, far):
    seq, width = dh.shape
    fq, fk = qr.shape[1], kr.shape[1]
    vmem = pl.BlockSpec(memory_space=pltpu.VMEM)
    flops = 2 * seq * width * (fq + fq + 2 * fk) + 10 * seq * seq * fq
    return pl.pallas_call(
        functools.partial(attend_back_kernel, far),
        out_shape=[
            jax.ShapeDtypeStruct((seq, fq + 2 * fk), BF),
            jax.ShapeDtypeStruct((seq // 2, width), BF),
            jax.ShapeDtypeStruct((seq // 2, width), BF),
        ],
        in_specs=[pl.BlockSpec(memory_space=pltpu.SMEM)] + [vmem] * 12,
        out_specs=[vmem] * 3,
        scratch_shapes=[
            pltpu.VMEM((seq, fq), BF),
            pltpu.VMEM((seq, fk), F32),
            pltpu.VMEM((seq, fk), F32),
        ],
        compiler_params=pltpu.CompilerParams(vmem_limit_bytes=LIMIT),
        cost_estimate=pl.CostEstimate(flops=flops, bytes_accessed=16 << 20, transcendentals=0),
        name="attend_back",
    )(me, dh, w_o, qr, kr, v, p, cos, sin, *weights)


def tables(places, width):
    halfway = width // 2
    counter = jnp.arange(halfway, dtype=jnp.float32)
    inverse = jnp.exp(counter * (-2.0 * math.log(THETA) / width))
    angles = places.astype(jnp.float32)[..., None] * inverse
    return (jnp.cos(angles), jnp.sin(angles))


def rms_scale(value_rows):
    return lax.rsqrt(jnp.mean(value_rows * value_rows, axis=-1, keepdims=True) + EPS)


def norm_back(grad_normed, unit_rows, recip_rows, gain_full):
    scaled = grad_normed * gain_full
    gain_grad = jnp.sum(grad_normed * unit_rows, axis=0)
    grad_rows = recip_rows * (
        scaled - unit_rows * jnp.mean(scaled * unit_rows, axis=-1, keepdims=True)
    )
    return (gain_grad, grad_rows)


def per_device(
    states,
    teacher,
    segments,
    positions,
    w_q,
    key_matrix,
    value_matrix,
    w_o,
    w_gate,
    w_up,
    w_down,
    norm1_gain,
    norm2_gain,
):
    net = Net()
    far = net.far
    seq, width = states.shape
    rp = w_q.shape[0]
    tok = seq // 4
    fq, fk = w_q.shape[1], key_matrix.shape[1]
    fqkv = fq + 2 * fk
    sub = w_gate.shape[1] // 4

    def blocks_at(a, n, places, axis):
        return jnp.concatenate(
            [lax.dynamic_slice_in_dim(a, at * n, n, axis) for at in places], axis=axis
        )

    def add(a, b):
        return (a.astype(F32) + b.astype(F32)).astype(BF)

    live = (segments > 0).astype(F32)
    alive = jnp.sum(live)
    high = jnp.floor(alive / 256.0)
    low = alive - high * 256.0
    rider = jnp.concatenate([norm1_gain, norm2_gain, jnp.zeros((fqkv - 2 * rp,), BF)])
    rider = jnp.stack([rider, jnp.pad(jnp.stack([high, low]).astype(BF), (0, fqkv - 2))])
    rider = jnp.pad(rider, ((0, EXTRA - 2), (0, 0)))
    qkv = jnp.concatenate(
        [jnp.concatenate([w_q, key_matrix, value_matrix], axis=1), rider], axis=0
    )
    qkv_own = jnp.stack(net.far_gather(qkv))

    def swap_y(w, axis):
        mine, other = [blocks_at(w, sub, [y, 2 + y], axis) for y in (net.y, 1 - net.y)]
        return in_order(net.y, mine, net.flip_y(other), 1 - axis)

    def swap_l(w, axis, *deps):
        mine, other = halves(net.l, w, axis)
        return in_order(net.l, mine, net.flip_l(after(other, *deps)), 1 - axis)

    def gather(w, axis):
        return lax.all_gather(
            w, "dp", axis=axis, axis_index_groups=net.far_groups, tiled=True
        )

    o_pair = in_order(net.y, w_o, net.flip_y(w_o), 1)
    gate = gather(swap_l(swap_y(w_gate, 1), 1), 0)
    up, down = swap_y(w_up, 1), swap_y(w_down, 0)

    qkv_l, qkv_y = net.flip_l(qkv_own), net.flip_y(qkv_own)
    o_far = net.absolute(net.far_gather(after(o_pair, qkv_own)), 1)
    qkv_all = (qkv_own, qkv_l, qkv_y, net.flip_y(qkv_l))
    o_l = net.flip_l(after(o_far, qkv_l))
    up = gather(swap_l(up, 1, qkv_l), 0)
    down = gather(swap_l(down, 0, qkv_all[3]), 1)
    parts = []
    for n in range(far):
        block = slice(n * 2 * rp, (n + 1) * 2 * rp)
        parts.append(in_order(net.l, o_far[:, block], o_l[:, block], 1))
    full_o = jnp.concatenate(parts, axis=1)

    me = jnp.stack([net.d, net.c]).astype(jnp.int32)
    cos_table, sin_table = tables(positions, HEAD_SIZE)
    normed, qr, kr, v, p, attended = attend(
        me, states, cos_table, sin_table, segments, qkv_all, fq, fk, far
    )
    rider = [w[k, rp : rp + 2] for w in qkv_all for k in range(far)]
    count = sum(e[1, 0].astype(F32) * 256.0 + e[1, 1].astype(F32) for e in rider)

    def gains(at):
        def piece(j, i, k):
            return qkv_all[2 * j + i][k, rp, at : at + rp].astype(F32)

        parts = []
        for k in range(far):
            pairs = [in_order(net.y, piece(0, i, k), piece(1, i, k), 0) for i in range(2)]
            parts.append(in_order(net.l, *pairs, 0))
        return net.absolute(parts, 0)[None, :]

    gain_one, gain_two = gains(0), gains(rp)

    def rows_of_core(a, which):
        return blocks_at(a, tok, [which, 2 + which], 0)

    send = net.flip_c(dot(rows_of_core(attended, 1 - net.c), full_o).astype(BF))
    keep = dot(rows_of_core(attended, net.c), full_o)
    keep, send = halves(net.x, keep + send.astype(F32), 0)
    attn_sum = keep + net.flip_x(send.astype(BF)).astype(F32)

    first_token = (net.x * 2 + net.c) * tok
    my_inputs = lax.dynamic_slice_in_dim(states, first_token, tok, 0).astype(F32)
    my_teacher = lax.dynamic_slice_in_dim(teacher, first_token, tok, 0).astype(F32)
    my_live = lax.dynamic_slice_in_dim(live, first_token, tok, 0)

    full_gate = jnp.concatenate([gate, net.flip_c(gate)], axis=1)
    full_up = jnp.concatenate([up, net.flip_c(up)], axis=1)
    full_down = jnp.concatenate([down, net.flip_c(down)], axis=0)
    hidden = my_inputs + attn_sum
    recip_two = rms_scale(hidden)
    unit_two = hidden * recip_two
    near, last = net.cube_gather((unit_two * gain_two).astype(BF))
    n2_near, n2_last = jnp.concatenate(near, axis=0), jnp.concatenate(last, axis=0)

    def act(n2):
        gate, up = dot(n2, full_gate), dot(n2, full_up)
        sig = jax.nn.sigmoid(gate)
        silu = gate * sig
        return (silu * up).astype(BF), up * sig * (1.0 + gate * (1.0 - sig)), silu

    act_near, by_gate_near, by_up_near = act(n2_near)
    act_last, by_gate_last, by_up_last = act(after(n2_last, act_near))
    y_last = dot(act_last, full_down).astype(BF)
    y_near = dot(after(act_near, y_last), full_down)
    mlp_sum = net.cube_reduce(split_parts(y_near, tok), split_parts(y_last, tok))
    output = hidden + mlp_sum
    error = (output - my_teacher) * my_live[:, None]
    factor = net.dp * seq / count
    grad_out = error * factor
    squares = jnp.sum(error * error)

    def share_tokens(a):
        a = in_order(net.x, a, net.flip_x(a), 0)
        b = net.flip_c(a)
        return jnp.concatenate(
            [in_order(net.c, a[:tok], b[:tok], 0), in_order(net.c, a[tok:], b[tok:], 0)], axis=0
        )

    near, last = net.cube_gather(grad_out.astype(BF))
    dy_all = jnp.concatenate(near + last, axis=0)
    act_all = jnp.concatenate([act_near, act_last], axis=0)
    n2_all = jnp.concatenate([n2_near, n2_last], axis=0)

    def sum_back(mine, other, axis):
        return lax.psum_scatter(
            add(mine, net.flip_c(other)),
            "dp",
            scatter_dimension=axis,
            axis_index_groups=net.far_groups,
            tiled=True,
        ).astype(F32)

    down_other = tn(act_all[:, sub:], dy_all).astype(BF)
    down_mine = tn(act_all[:, :sub], dy_all).astype(BF)
    down_sum = sum_back(down_mine, down_other, 1)
    grad_active = nt(after(dy_all, down_mine), full_down)
    dg_all = (grad_active * jnp.concatenate([by_gate_near, by_gate_last], axis=0)).astype(BF)
    du_all = (grad_active * jnp.concatenate([by_up_near, by_up_last], axis=0)).astype(BF)
    dn_all = nt(dg_all, full_gate) + nt(du_all, full_up)
    dn_near, dn_last = dn_all[: 4 * tok], dn_all[4 * tok :].astype(BF)
    n2_all, dg_late, du_late = after((n2_all, dg_all, du_all), dn_last)
    gate_other = tn(n2_all, dg_late[:, sub:]).astype(BF)
    gate_mine = tn(n2_all, dg_late[:, :sub]).astype(BF)
    gate_sum = sum_back(gate_mine, gate_other, 0)
    up_other = tn(n2_all, du_late[:, sub:]).astype(BF)
    up_mine = tn(n2_all, du_late[:, :sub]).astype(BF)
    up_sum = sum_back(up_mine, up_other, 0)

    back_two = net.cube_reduce(split_parts(dn_near, tok), split_parts(dn_last, tok))
    gain_two_grad, hidden_from_norm = norm_back(back_two, unit_two, recip_two, gain_two)
    grad_hidden = grad_out + hidden_from_norm
    grad_hidden_low = share_tokens(grad_hidden.astype(BF))
    out_states = share_tokens(after(output.astype(BF), grad_hidden_low))

    grad_qkv, send, keep = attend_back(
        me, grad_hidden_low, full_o, qr, kr, v, p, cos_table, sin_table, qkv_all, far
    )
    back_one = (keep.astype(F32) + net.flip_c(send).astype(F32)).astype(BF)
    back_got = net.flip_x(back_one)
    dh_low, att, n1, g_qkv = after((grad_hidden_low, attended, normed, grad_qkv), send)
    grad_wqkv = tn(n1, g_qkv).astype(BF)
    grad_wo = tn(att, dh_low).astype(BF)

    half, quarter = width // 2, width // 4
    gq, gkv = grad_wqkv[:, :fq], grad_wqkv[:, fq:]
    gkv = [gkv[n * quarter : (n + 1) * quarter] for n in range(4)]
    q_got = net.flip_y(gq[half:])
    kv_got = net.flip_l(jnp.concatenate([gkv[1], gkv[3]], axis=0))
    q_got, kv_got, back_got = pin(q_got, kv_got, back_got)
    gq = add(gq[:half], q_got)
    gkv = add(jnp.concatenate([gkv[0], gkv[2]], axis=0), kv_got)
    q_got = net.flip_l(gq[quarter:])
    kv_got = net.flip_y(gkv[quarter:])
    gqkv = jnp.concatenate([add(gq[:quarter], q_got), add(gkv[:quarter], kv_got)], axis=1)

    other = blocks_at(grad_wo, rp, [2 * n + 1 - net.y for n in range(2 * far)], 1)
    go = add(
        blocks_at(grad_wo, rp, [2 * n + net.y for n in range(2 * far)], 1), net.flip_y(other)
    )
    other = blocks_at(go, rp, [2 * n + 1 - net.l for n in range(far)], 1)
    go = add(blocks_at(go, rp, [2 * n + net.l for n in range(far)], 1), net.flip_l(other))

    def far_blocks(a):
        n = a.shape[0] // far
        return [a[k * n : (k + 1) * n] for k in range(far)]

    go = [
        lax.dynamic_slice_in_dim(go, jnp.bitwise_xor(net.f, k) * rp, rp, 1) for k in range(far)
    ]
    result_qkv = net.far_reduce(far_blocks(gqkv)).astype(F32)
    result_o = net.far_reduce(go).astype(F32)
    result_q = result_qkv[:, :fq]
    result_k, result_v = result_qkv[:, fq : fq + fk], result_qkv[:, fq + fk :]

    def exchange(total, axis):
        cross = 1 - axis
        mine, other = halves(net.l, total, axis)
        got = net.flip_l(other.astype(BF)).astype(F32)
        mine, other = halves(net.y, in_order(net.l, mine, got, cross), axis)
        got = net.flip_y(other.astype(BF)).astype(F32)
        parts = []
        for n in range(2):
            cut = functools.partial(
                lax.slice_in_dim, start_index=n * sub, limit_index=(n + 1) * sub, axis=cross
            )
            parts.append(in_order(net.y, cut(mine), cut(got), cross))
        return jnp.concatenate(parts, axis=cross)

    result_down = exchange(after(down_sum, send), 1)
    result_gate = exchange(after(gate_sum, back_got), 0)
    result_up = exchange(after(up_sum, back_got), 0)

    back_one = back_one.astype(F32) + back_got.astype(F32)
    xf = rows_of_core(states, net.c).astype(F32)
    recip_mine = rms_scale(xf)
    gain_one_grad, from_norm = norm_back(back_one, xf * recip_mine, recip_mine, gain_one)
    grad_input = rows_of_core(grad_hidden_low, net.c).astype(F32) + from_norm
    grad_other = net.flip_c(grad_input)
    grad_input = jnp.concatenate(
        [
            in_order(net.c, grad_input[:tok], grad_other[:tok], 0),
            in_order(net.c, grad_input[tok:], grad_other[tok:], 0),
        ],
        axis=0,
    )

    small = jnp.concatenate([0.5 * gain_one_grad, gain_two_grad, jnp.full((128,), squares, F32)])
    small = small.reshape(-1, 128)
    small = small + net.flip_c(small)
    small = small + net.flip_x(small)
    small = net.dp_sum(small).reshape(-1)
    result_g1 = lax.dynamic_slice_in_dim(small[:width], net.d * rp, rp)
    result_g2 = lax.dynamic_slice_in_dim(small[width : 2 * width], net.d * rp, rp)
    loss_value = small[2 * width] / (count * width)
    return (
        out_states,
        grad_input,
        loss_value,
        result_q,
        result_k,
        result_v,
        result_o,
        result_gate,
        result_up,
        result_down,
        result_g1,
        result_g2,
    )


def solution(mesh):
    in_specs = (
        P("dp", None),
        P("dp", None),
        P("dp"),
        P("dp"),
        P("dp", "tensor"),
        P("dp", "tensor"),
        P("dp", "tensor"),
        P("tensor", "dp"),
        P("dp", "tensor"),
        P("dp", "tensor"),
        P("tensor", "dp"),
        P("dp"),
        P("dp"),
    )
    out_specs = (
        P("dp", None),
        P("dp", None),
        P(),
        P("dp", "tensor"),
        P("dp", "tensor"),
        P("dp", "tensor"),
        P("tensor", "dp"),
        P("dp", "tensor"),
        P("dp", "tensor"),
        P("tensor", "dp"),
        P("dp"),
        P("dp"),
    )
    return jax.shard_map(
        per_device, mesh=mesh, in_specs=in_specs, out_specs=out_specs, check_vma=False
    )
```

```python
import functools
import math

import jax
import jax.numpy as jnp
from jax import lax
from jax.experimental import pallas as pl
from jax.experimental.pallas import tpu as pltpu
from jax.sharding import PartitionSpec as P

HEAD_SIZE = 256

EPS = 1e-06
THETA = 1000042.0
AXES = ("dp", "tensor")
BF = jnp.bfloat16
F32 = jnp.float32
EXTRA = 16
LIMIT = 56 * 1024 * 1024


class Net:
    def __init__(self):
        self.dp = lax.axis_size("dp")
        self.tensor = lax.axis_size("tensor")
        self.bits = self.dp.bit_length() - 1
        self.far = self.dp // 4
        self.d = lax.axis_index("dp")
        t = lax.axis_index("tensor")
        self.y, self.l, self.f = self.d % 2, (self.d // 2) % 2, self.d // 4
        self.x, self.c = t // 2, t % 2
        self.near_groups = [[4 * f + low for low in range(4)] for f in range(self.far)]
        self.far_groups = [[4 * f + low for f in range(self.far)] for low in range(4)]

    def flip(self, v, dp_mask, tensor_mask=0):
        pairs = []
        for d in range(self.dp):
            for t in range(self.tensor):
                there = (d ^ dp_mask) * self.tensor + (t ^ tensor_mask)
                pairs.append((d * self.tensor + t, there))
        return lax.ppermute(v, AXES, pairs)

    def flip_y(self, v):
        return self.flip(v, 1)

    def flip_l(self, v):
        return self.flip(v, 2)

    def flip_x(self, v):
        return self.flip(v, 0, 2)

    def flip_c(self, v):
        return self.flip(v, 0, 1)

    def dp_sum(self, v):
        for bit in range(self.bits):
            v = v + self.flip(v, 1 << bit)
        return v

    def far_gather(self, v):
        pieces = [v]
        bit = 4
        while bit < self.dp:
            sent = pieces[0] if len(pieces) == 1 else jnp.stack(pieces)
            got = self.flip(sent, bit)
            pieces = pieces + ([got] if len(pieces) == 1 else [got[k] for k in range(len(pieces))])
            bit *= 2
        return pieces

    def absolute(self, pieces, axis):
        if self.far == 2:
            return in_order(self.f, *pieces, axis)
        stack = jnp.stack(pieces)
        return jnp.concatenate(
            [
                lax.dynamic_index_in_dim(stack, jnp.bitwise_xor(self.f, n), 0, keepdims=False)
                for n in range(self.far)
            ],
            axis=axis,
        )

    def far_reduce(self, pieces, *deps):
        bit = self.dp // 2
        while bit >= 4:
            n = len(pieces) // 2
            sent = pieces[n:]
            got = self.flip(sent[0] if n == 1 else jnp.stack(sent), bit)
            got = after(got, *deps) if deps else got
            got = [got] if n == 1 else [got[k] for k in range(n)]
            pieces = [
                p.astype(F32) + g.astype(F32) if n == 1 else (p.astype(F32) + g.astype(F32)).astype(BF)
                for p, g in zip(pieces[:n], got)
            ]
            bit //= 2
        return pieces[0]

    def cube_gather(self, v):
        parts = [v[a:b] for a, b in part_rows(v.shape[0])]
        for step in range(2):
            got = [self.cube_flip(n, step, part) for n, part in enumerate(parts)]
            parts = [jnp.concatenate(pair, axis=0) for pair in zip(parts, got)]
        last = [self.cube_flip(n, 2, part) for n, part in enumerate(parts)]
        return parts, last

    def cube_flip(self, part, step, v):
        return (self.flip_l, self.flip_y, self.flip_x)[(part + step) % 3](v)

    def cube_reduce(self, near, last):
        got = [self.cube_flip(n, 2, v.astype(BF)) for n, v in enumerate(last)]
        parts = [a.astype(F32) + b.astype(F32) for a, b in zip(near, got)]
        for step in (1, 0):
            half = [v.shape[0] // 2 for v in parts]
            got = [
                self.cube_flip(n, step, v[h:].astype(BF)) for n, (v, h) in enumerate(zip(parts, half))
            ]
            parts = [v[:h] + g.astype(F32) for v, h, g in zip(parts, half, got)]
        return jnp.concatenate(parts, axis=0)


def part_rows(n):
    one = -(-n // 48) * 16
    return [(0, one), (one, 2 * one), (2 * one, n)]


def split_parts(v, n):
    out, at = [], 0
    for a, b in part_rows(n):
        out.append(v[at : at + 4 * (b - a)])
        at += 4 * (b - a)
    return out


def in_order(flag, mine, other, axis):
    first = jnp.where(flag == 0, mine, other)
    second = jnp.where(flag == 0, other, mine)
    return jnp.concatenate([first, second], axis=axis)


def halves(flag, v, axis):
    n = v.shape[axis] // 2
    mine = lax.dynamic_slice_in_dim(v, flag * n, n, axis)
    other = lax.dynamic_slice_in_dim(v, (1 - flag) * n, n, axis)
    return mine, other


def after(value, *deps):
    return lax.optimization_barrier((value,) + deps)[0]


def pin(*values):
    return lax.optimization_barrier(values)


def nt(left, right):
    return lax.dot_general(left, right, (((1,), (1,)), ((), ())), preferred_element_type=F32)


def tn(left, right):
    return lax.dot_general(left, right, (((0,), (0,)), ((), ())), preferred_element_type=F32)


def dot(left, right):
    return jnp.dot(left, right, preferred_element_type=F32)


def spin(v, cos, sin):
    half = v.shape[-1] // 2
    a, b = v[:, :half], v[:, half:]
    return jnp.concatenate([a * cos - b * sin, b * cos + a * sin], axis=-1)


def attend_kernel(far, *refs):
    me, states, cos_ref, sin_ref, seg_col, seg_row, *weights = refs[:10]
    n1_ref, qr_ref, kr_ref, v_ref, p_ref, o_ref = refs[10:]
    seq, width = states.shape
    rp = width // (4 * far)
    fq, fk = qr_ref.shape[1], kr_ref.shape[1]
    tile = min(128, seq)
    scale = 1.0 / math.sqrt(HEAD_SIZE)
    d = me[0]

    @pl.loop(0, seq // tile)
    def _(number):
        rows = pl.ds(pl.multiple_of(number * tile, tile), tile)
        xf = states[rows, :].astype(F32)
        recip = lax.rsqrt(jnp.mean(xf * xf, axis=-1, keepdims=True) + EPS)
        total = None
        for j in range(2):
            for i in range(2):
                for k in range(far):
                    at = jnp.bitwise_xor(d, 4 * k + 2 * i + j)
                    if rp % 128 == 0:
                        block = states[rows, pl.ds(pl.multiple_of(at * rp, 128), rp)].astype(F32)
                    else:
                        first = pl.multiple_of((at // 2) * (2 * rp), 128)
                        block = states[rows, pl.ds(first, 2 * rp)].astype(F32)
                        block = jnp.where(at % 2 == 0, block[:, :rp], block[:, rp:])
                    w = weights[2 * j + i]
                    gain = w[k, rp : rp + EXTRA, :rp][:1].astype(F32)
                    normed = (block * recip * gain).astype(BF)
                    place = ((j * 2 + i) * far + k) * rp
                    n1_ref[rows, place : place + rp] = normed
                    part = dot(normed, w[k, :rp, :])
                    total = part if total is None else total + part
        cos, sin = cos_ref[rows, :], sin_ref[rows, :]
        for head in range(fq // HEAD_SIZE):
            block = slice(head * HEAD_SIZE, (head + 1) * HEAD_SIZE)
            qr_ref[rows, block] = spin(total[:, block], cos, sin).astype(BF)
        for head in range(fk // HEAD_SIZE):
            block = slice(head * HEAD_SIZE, (head + 1) * HEAD_SIZE)
            at = fq + head * HEAD_SIZE
            kr_ref[rows, block] = spin(total[:, at : at + HEAD_SIZE], cos, sin).astype(BF)
        v_ref[rows, :] = total[:, fq + fk :].astype(BF)

    rep = fq // fk
    for i in range(seq // tile):
        rows, keys = slice(i * tile, (i + 1) * tile), slice(0, (i + 1) * tile)
        shape = (tile, (i + 1) * tile)
        behind = lax.broadcasted_iota(jnp.int32, shape, 1) <= (
            lax.broadcasted_iota(jnp.int32, shape, 0) + i * tile
        )
        allowed = (seg_col[rows, :] == seg_row[:, keys]) & behind
        for head in range(fq // HEAD_SIZE):
            block = slice(head * HEAD_SIZE, (head + 1) * HEAD_SIZE)
            k = head // rep
            kblock = slice(k * HEAD_SIZE, (k + 1) * HEAD_SIZE)
            s = nt(qr_ref[rows, block], kr_ref[keys, kblock]) * scale
            s = jnp.where(allowed, s, -1e30)
            e = jnp.exp(s - jnp.max(s, axis=-1, keepdims=True))
            p = (e / jnp.sum(e, axis=-1, keepdims=True)).astype(BF)
            p_ref[head, rows, keys] = p
            o_ref[rows, block] = dot(p, v_ref[keys, kblock]).astype(BF)


def attend(me, states, cos, sin, segments, weights, fq, fk, far):
    seq, width = states.shape
    shapes = [
        jax.ShapeDtypeStruct((seq, width), BF),
        jax.ShapeDtypeStruct((seq, fq), BF),
        jax.ShapeDtypeStruct((seq, fk), BF),
        jax.ShapeDtypeStruct((seq, fk), BF),
        jax.ShapeDtypeStruct((fq // HEAD_SIZE, seq, seq), BF),
        jax.ShapeDtypeStruct((seq, fq), BF),
    ]
    vmem = pl.BlockSpec(memory_space=pltpu.VMEM)
    flops = 2 * seq * width * (fq + 2 * fk) + 4 * seq * seq * fq
    return pl.pallas_call(
        functools.partial(attend_kernel, far),
        out_shape=shapes,
        in_specs=[pl.BlockSpec(memory_space=pltpu.SMEM)] + [vmem] * 9,
        out_specs=[vmem] * 6,
        compiler_params=pltpu.CompilerParams(vmem_limit_bytes=LIMIT),
        cost_estimate=pl.CostEstimate(
            flops=flops, bytes_accessed=12 << 20, transcendentals=seq * seq * 2
        ),
        name="attend",
    )(me, states, cos, sin, segments[:, None], segments[None, :], *weights)


def attend_back_kernel(far, *refs):
    me, dh, w_o, qr_ref, kr_ref, v_ref, p_ref, cos_ref, sin_ref, *weights = refs[:13]
    d_ref, send_ref, keep_ref = refs[13:16]
    do_ref, dk_ref, dv_ref = refs[16:]
    seq, width = dh.shape
    rp = width // (4 * far)
    fq, fk = qr_ref.shape[1], kr_ref.shape[1]
    tile = min(128, seq)
    scale = 1.0 / math.sqrt(HEAD_SIZE)
    rep = fq // fk

    @pl.loop(0, seq // tile)
    def _(i):
        rows = pl.ds(pl.multiple_of(i * tile, tile), tile)
        do_ref[rows, :] = nt(dh[rows, :], w_o[...]).astype(BF)

    dk_ref[...] = jnp.zeros_like(dk_ref)
    dv_ref[...] = jnp.zeros_like(dv_ref)
    for i in range(seq // tile):
        rows, keys = slice(i * tile, (i + 1) * tile), slice(0, (i + 1) * tile)
        cos, sin = cos_ref[rows, :], -sin_ref[rows, :]
        for head in range(fq // HEAD_SIZE):
            block = slice(head * HEAD_SIZE, (head + 1) * HEAD_SIZE)
            k = head // rep
            kblock = slice(k * HEAD_SIZE, (k + 1) * HEAD_SIZE)
            do = do_ref[rows, block]
            pb = p_ref[head, rows, keys]
            p = pb.astype(F32)
            dp = nt(do, v_ref[keys, kblock])
            inner = jnp.sum(p * dp, axis=-1, keepdims=True)
            ds = (p * (dp - inner)).astype(BF)
            dq = dot(ds, kr_ref[keys, kblock]) * scale
            d_ref[rows, block] = spin(dq, cos, sin).astype(BF)
            dk_ref[keys, kblock] += tn(ds, qr_ref[rows, block])
            dv_ref[keys, kblock] += tn(pb, do)
    for head in range(fk // HEAD_SIZE):
        block = slice(head * HEAD_SIZE, (head + 1) * HEAD_SIZE)
        at = fq + head * HEAD_SIZE
        d_ref[:, at : at + HEAD_SIZE] = spin(
            dk_ref[:, block] * scale, cos_ref[...], -sin_ref[...]
        ).astype(BF)
    d_ref[:, fq + fk :] = dv_ref[...].astype(BF)

    tok = seq // 4
    mine, d = me[1], me[0]
    for side in range(2):
        out = slice(side * tok, (side + 1) * tok)
        for ref, which in ((send_ref, 1 - mine), (keep_ref, mine)):
            rows = pl.ds(pl.multiple_of((side * 2 + which) * tok, tok), tok)
            grad = d_ref[rows, :]
            for i in range(2):
                for k in range(far):
                    values = [
                        nt(grad, weights[2 * j + i][k, :rp, :]).astype(BF) for j in range(2)
                    ]
                    at = jnp.bitwise_xor(d, 4 * k + 2 * i)
                    if rp % 128 == 0:
                        for j in range(2):
                            place = pl.multiple_of(jnp.bitwise_xor(at, j) * rp, 128)
                            ref[out, pl.ds(place, rp)] = values[j]
                    else:
                        place = pl.multiple_of((at // 2) * (2 * rp), 128)
                        pair = [jnp.concatenate(v, axis=-1) for v in (values, values[::-1])]
                        ref[out, pl.ds(place, 2 * rp)] = jnp.where(at % 2 == 0, *pair)


def attend_back(me, dh, w_o, qr, kr, v, p, cos, sin, weights, far):
    seq, width = dh.shape
    fq, fk = qr.shape[1], kr.shape[1]
    vmem = pl.BlockSpec(memory_space=pltpu.VMEM)
    flops = 2 * seq * width * (fq + fq + 2 * fk) + 10 * seq * seq * fq
    return pl.pallas_call(
        functools.partial(attend_back_kernel, far),
        out_shape=[
            jax.ShapeDtypeStruct((seq, fq + 2 * fk), BF),
            jax.ShapeDtypeStruct((seq // 2, width), BF),
            jax.ShapeDtypeStruct((seq // 2, width), BF),
        ],
        in_specs=[pl.BlockSpec(memory_space=pltpu.SMEM)] + [vmem] * 12,
        out_specs=[vmem] * 3,
        scratch_shapes=[
            pltpu.VMEM((seq, fq), BF),
            pltpu.VMEM((seq, fk), F32),
            pltpu.VMEM((seq, fk), F32),
        ],
        compiler_params=pltpu.CompilerParams(vmem_limit_bytes=LIMIT),
        cost_estimate=pl.CostEstimate(flops=flops, bytes_accessed=16 << 20, transcendentals=0),
        name="attend_back",
    )(me, dh, w_o, qr, kr, v, p, cos, sin, *weights)


def tables(places, width):
    halfway = width // 2
    counter = jnp.arange(halfway, dtype=jnp.float32)
    inverse = jnp.exp(counter * (-2.0 * math.log(THETA) / width))
    angles = places.astype(jnp.float32)[..., None] * inverse
    return (jnp.cos(angles), jnp.sin(angles))


def rms_scale(value_rows):
    return lax.rsqrt(jnp.mean(value_rows * value_rows, axis=-1, keepdims=True) + EPS)


def norm_back(grad_normed, unit_rows, recip_rows, gain_full):
    scaled = grad_normed * gain_full
    gain_grad = jnp.sum(grad_normed * unit_rows, axis=0)
    grad_rows = recip_rows * (
        scaled - unit_rows * jnp.mean(scaled * unit_rows, axis=-1, keepdims=True)
    )
    return (gain_grad, grad_rows)


def per_device(
    states,
    teacher,
    segments,
    positions,
    w_q,
    key_matrix,
    value_matrix,
    w_o,
    w_gate,
    w_up,
    w_down,
    norm1_gain,
    norm2_gain,
):
    net = Net()
    far = net.far
    seq, width = states.shape
    rp = w_q.shape[0]
    tok = seq // 4
    fq, fk = w_q.shape[1], key_matrix.shape[1]
    fqkv = fq + 2 * fk
    sub = w_gate.shape[1] // 4

    def blocks_at(a, n, places, axis):
        return jnp.concatenate(
            [lax.dynamic_slice_in_dim(a, at * n, n, axis) for at in places], axis=axis
        )

    def add(a, b):
        return (a.astype(F32) + b.astype(F32)).astype(BF)

    live = (segments > 0).astype(F32)
    alive = jnp.sum(live)
    high = jnp.floor(alive / 256.0)
    low = alive - high * 256.0
    rider = jnp.concatenate([norm1_gain, norm2_gain, jnp.zeros((fqkv - 2 * rp,), BF)])
    rider = jnp.stack([rider, jnp.pad(jnp.stack([high, low]).astype(BF), (0, fqkv - 2))])
    rider = jnp.pad(rider, ((0, EXTRA - 2), (0, 0)))
    qkv = jnp.concatenate(
        [jnp.concatenate([w_q, key_matrix, value_matrix], axis=1), rider], axis=0
    )

    def exchange(w, split, concat):
        return lax.all_to_all(
            w, "dp", split, concat, axis_index_groups=net.near_groups, tiled=True
        )

    def gather(w, axis):
        return lax.all_gather(
            w, "dp", axis=axis, axis_index_groups=net.far_groups, tiled=True
        )

    w_gate, w_up, w_down = after((w_gate, w_up, w_down), qkv)
    o_pair = in_order(net.y, w_o, net.flip_y(w_o), 1)
    qkv_own = jnp.stack(net.far_gather(qkv))
    gate = exchange(w_gate, 1, 0)
    up = exchange(after(w_up, gate), 1, 0)
    down = exchange(after(w_down, up), 0, 1)
    gate = gather(gate, 0)
    qkv_l, qkv_y = net.flip_l(qkv_own), net.flip_y(qkv_own)
    o_far = net.far_gather(after(o_pair, qkv_own))
    o_far = net.absolute([after(o, qkv_l, qkv_y) for o in o_far], 1)
    o_l = net.flip_l(o_far)
    qkv_ly, up = pin(net.flip_y(qkv_l), up)
    up = gather(up, 0)
    qkv_ly, gate = pin(qkv_ly, gate)
    qkv_all = (qkv_own, qkv_l, qkv_y, qkv_ly)

    me = jnp.stack([net.d, net.c]).astype(jnp.int32)
    cos_table, sin_table = tables(positions, HEAD_SIZE)
    normed, qr, kr, v, p, attended = attend(
        me, states, cos_table, sin_table, segments, qkv_all, fq, fk, far
    )
    o_l = after(o_l, attended)
    parts = []
    for n in range(far):
        block = slice(n * 2 * rp, (n + 1) * 2 * rp)
        parts.append(in_order(net.l, o_far[:, block], o_l[:, block], 1))
    full_o = jnp.concatenate(parts, axis=1)

    rider = [w[k, rp : rp + 2] for w in qkv_all for k in range(far)]
    count = sum(e[1, 0].astype(F32) * 256.0 + e[1, 1].astype(F32) for e in rider)

    def gains(at):
        def piece(j, i, k):
            return qkv_all[2 * j + i][k, rp, at : at + rp].astype(F32)

        parts = []
        for k in range(far):
            pairs = [in_order(net.y, piece(0, i, k), piece(1, i, k), 0) for i in range(2)]
            parts.append(in_order(net.l, *pairs, 0))
        return net.absolute(parts, 0)[None, :]

    gain_one, gain_two = gains(0), gains(rp)

    def rows_of_core(a, which):
        return blocks_at(a, tok, [which, 2 + which], 0)

    send = net.flip_c(dot(rows_of_core(attended, 1 - net.c), full_o).astype(BF))
    keep = dot(rows_of_core(attended, net.c), full_o)
    keep, send = halves(net.x, keep + send.astype(F32), 0)
    attn_sum = keep + net.flip_x(send.astype(BF)).astype(F32)

    first_token = (net.x * 2 + net.c) * tok
    my_inputs = lax.dynamic_slice_in_dim(states, first_token, tok, 0).astype(F32)
    my_teacher = lax.dynamic_slice_in_dim(teacher, first_token, tok, 0).astype(F32)
    my_live = lax.dynamic_slice_in_dim(live, first_token, tok, 0)

    attn_sum, down = pin(attn_sum, down)
    down = gather(down, 1)
    full_gate = jnp.concatenate([gate, net.flip_c(gate)], axis=1)
    hidden = my_inputs + attn_sum
    recip_two = rms_scale(hidden)
    unit_two = hidden * recip_two
    near, last = net.cube_gather((unit_two * gain_two).astype(BF))
    up = after(up, *near)
    full_up = jnp.concatenate([up, net.flip_c(up)], axis=1)
    n2_near, n2_last = jnp.concatenate(near, axis=0), jnp.concatenate(last, axis=0)

    def act(n2):
        gate, up = dot(n2, full_gate), dot(n2, full_up)
        sig = jax.nn.sigmoid(gate)
        silu = gate * sig
        by_gate = (up * sig * (1.0 + gate * (1.0 - sig))).astype(BF)
        return (silu * up).astype(BF), by_gate, silu.astype(BF)

    act_near, by_gate_near, by_up_near = act(n2_near)
    act_last, by_gate_last, by_up_last = act(after(n2_last, act_near))
    down = after(down, act_last)
    full_down = jnp.concatenate([down, net.flip_c(down)], axis=0)
    y_last = dot(act_last, full_down).astype(BF)
    y_near = dot(after(act_near, y_last), full_down)
    mlp_sum = net.cube_reduce(split_parts(y_near, tok), split_parts(y_last, tok))
    output = hidden + mlp_sum
    error = (output - my_teacher) * my_live[:, None]
    factor = net.dp * seq / count
    grad_out = error * factor
    squares = jnp.sum(error * error)

    def share_tokens(a):
        a = in_order(net.x, a, net.flip_x(a), 0)
        b = net.flip_c(a)
        return jnp.concatenate(
            [in_order(net.c, a[:tok], b[:tok], 0), in_order(net.c, a[tok:], b[tok:], 0)], axis=0
        )

    near, last = net.cube_gather(grad_out.astype(BF))
    dy_all = jnp.concatenate(near + last, axis=0)
    act_all = jnp.concatenate([act_near, act_last], axis=0)
    n2_all = jnp.concatenate([n2_near, n2_last], axis=0)

    def sum_back(total, axis):
        return lax.psum_scatter(
            total, "dp", scatter_dimension=axis, axis_index_groups=net.far_groups, tiled=True
        )

    down_other = tn(act_all[:, sub:], dy_all).astype(BF)
    down_mine = tn(act_all[:, :sub], dy_all).astype(BF)
    down_got = net.flip_c(down_other)
    grad_active = nt(after(dy_all, down_mine), full_down)
    dg_all = (grad_active * jnp.concatenate([by_gate_near, by_gate_last], axis=0)).astype(BF)
    du_all = (grad_active * jnp.concatenate([by_up_near, by_up_last], axis=0)).astype(BF)
    dg_all, du_all, down_sum = pin(dg_all, du_all, add(down_mine, down_got))
    down_sum = sum_back(down_sum, 1)
    dn_all = nt(dg_all, full_gate) + nt(du_all, full_up)
    dn_near, dn_last = dn_all[: 4 * tok], dn_all[4 * tok :].astype(BF)
    n2_all, dg_late, du_late = after((n2_all, dg_all, du_all), dn_last)
    gate_other = tn(n2_all, dg_late[:, sub:]).astype(BF)
    gate_mine = tn(n2_all, dg_late[:, :sub]).astype(BF)
    gate_sum = sum_back(add(gate_mine, net.flip_c(gate_other)), 0)
    up_other = tn(n2_all, du_late[:, sub:]).astype(BF)
    up_mine = tn(n2_all, du_late[:, :sub]).astype(BF)
    up_sum = sum_back(add(up_mine, net.flip_c(up_other)), 0)

    back_two = net.cube_reduce(split_parts(dn_near, tok), split_parts(dn_last, tok))
    gain_two_grad, hidden_from_norm = norm_back(back_two, unit_two, recip_two, gain_two)
    grad_hidden = grad_out + hidden_from_norm
    grad_hidden_low = share_tokens(grad_hidden.astype(BF))
    out_states = share_tokens(after(output.astype(BF), grad_hidden_low))

    grad_qkv, send, keep = attend_back(
        me, grad_hidden_low, full_o, qr, kr, v, p, cos_table, sin_table, qkv_all, far
    )
    back_one = (keep.astype(F32) + net.flip_c(send).astype(F32)).astype(BF)
    back_got = net.flip_x(back_one)
    dh_low, att, n1, g_qkv = after((grad_hidden_low, attended, normed, grad_qkv), send)
    grad_wqkv = tn(n1, g_qkv).astype(BF)
    grad_wo = tn(att, dh_low).astype(BF)

    half, quarter = width // 2, width // 4
    gq, gkv = grad_wqkv[:, :fq], grad_wqkv[:, fq:]
    gkv = [gkv[n * quarter : (n + 1) * quarter] for n in range(4)]
    q_got = net.flip_y(gq[half:])
    kv_got = net.flip_l(jnp.concatenate([gkv[1], gkv[3]], axis=0))
    q_got, gate_sum = pin(q_got, gate_sum)
    q_got, kv_got, back_got = pin(q_got, kv_got, back_got)
    gq = add(gq[:half], q_got)
    gkv = add(jnp.concatenate([gkv[0], gkv[2]], axis=0), kv_got)
    q_got = net.flip_l(gq[quarter:])
    kv_got = net.flip_y(gkv[quarter:])
    q_got, kv_got, up_sum = pin(q_got, kv_got, up_sum)
    gqkv = jnp.concatenate([add(gq[:quarter], q_got), add(gkv[:quarter], kv_got)], axis=1)

    other = blocks_at(grad_wo, rp, [2 * n + 1 - net.y for n in range(2 * far)], 1)
    go = add(
        blocks_at(grad_wo, rp, [2 * n + net.y for n in range(2 * far)], 1), net.flip_y(other)
    )
    other = blocks_at(go, rp, [2 * n + 1 - net.l for n in range(far)], 1)
    go = add(blocks_at(go, rp, [2 * n + net.l for n in range(far)], 1), net.flip_l(other))

    def far_blocks(a):
        n = a.shape[0] // far
        return [a[k * n : (k + 1) * n] for k in range(far)]

    go = [
        lax.dynamic_slice_in_dim(go, jnp.bitwise_xor(net.f, k) * rp, rp, 1) for k in range(far)
    ]
    result_qkv = net.far_reduce(far_blocks(gqkv)).astype(F32)
    result_o = net.far_reduce(go).astype(F32)
    result_q = result_qkv[:, :fq]
    result_k, result_v = result_qkv[:, fq : fq + fk], result_qkv[:, fq + fk :]

    result_down = exchange(after(down_sum, send), 1, 0).astype(F32)
    result_gate = exchange(after(gate_sum, back_got), 0, 1).astype(F32)
    result_up = exchange(after(up_sum, far_blocks(gqkv)[0]), 0, 1).astype(F32)

    back_one = back_one.astype(F32) + back_got.astype(F32)
    xf = rows_of_core(states, net.c).astype(F32)
    recip_mine = rms_scale(xf)
    gain_one_grad, from_norm = norm_back(back_one, xf * recip_mine, recip_mine, gain_one)
    grad_input = rows_of_core(grad_hidden_low, net.c).astype(F32) + from_norm
    grad_other = net.flip_c(grad_input)
    grad_input = jnp.concatenate(
        [
            in_order(net.c, grad_input[:tok], grad_other[:tok], 0),
            in_order(net.c, grad_input[tok:], grad_other[tok:], 0),
        ],
        axis=0,
    )

    small = jnp.concatenate([0.5 * gain_one_grad, gain_two_grad, jnp.full((128,), squares, F32)])
    small = small.reshape(-1, 128)
    small = small + net.flip_c(small)
    small = small + net.flip_x(small)
    small = net.dp_sum(small).reshape(-1)
    result_g1 = lax.dynamic_slice_in_dim(small[:width], net.d * rp, rp)
    result_g2 = lax.dynamic_slice_in_dim(small[width : 2 * width], net.d * rp, rp)
    loss_value = small[2 * width] / (count * width)
    return (
        out_states,
        grad_input,
        loss_value,
        result_q,
        result_k,
        result_v,
        result_o,
        result_gate,
        result_up,
        result_down,
        result_g1,
        result_g2,
    )


def solution(mesh):
    in_specs = (
        P("dp", None),
        P("dp", None),
        P("dp"),
        P("dp"),
        P("dp", "tensor"),
        P("dp", "tensor"),
        P("dp", "tensor"),
        P("tensor", "dp"),
        P("dp", "tensor"),
        P("dp", "tensor"),
        P("tensor", "dp"),
        P("dp"),
        P("dp"),
    )
    out_specs = (
        P("dp", None),
        P("dp", None),
        P(),
        P("dp", "tensor"),
        P("dp", "tensor"),
        P("dp", "tensor"),
        P("tensor", "dp"),
        P("dp", "tensor"),
        P("dp", "tensor"),
        P("tensor", "dp"),
        P("dp"),
        P("dp"),
    )
    return jax.shard_map(
        per_device, mesh=mesh, in_specs=in_specs, out_specs=out_specs, check_vma=False
    )
```

```python
import functools
import math

import jax
import jax.numpy as jnp
from jax import lax
from jax.experimental import pallas as pl
from jax.experimental.pallas import tpu as pltpu
from jax.sharding import PartitionSpec as P

HEAD_SIZE = 256

EPS = 1e-06
THETA = 1000042.0
AXES = ("dp", "tensor")
BF = jnp.bfloat16
F32 = jnp.float32
EXTRA = 16
LIMIT = 56 * 1024 * 1024


class Net:
    def __init__(self):
        self.dp = lax.axis_size("dp")
        self.tensor = lax.axis_size("tensor")
        self.bits = self.dp.bit_length() - 1
        self.far = self.dp // 4
        self.d = lax.axis_index("dp")
        t = lax.axis_index("tensor")
        self.y, self.l, self.f = self.d % 2, (self.d // 2) % 2, self.d // 4
        self.x, self.c = t // 2, t % 2
        self.near_groups = [[4 * f + low for low in range(4)] for f in range(self.far)]
        self.far_groups = [[4 * f + low for f in range(self.far)] for low in range(4)]

    def flip(self, v, dp_mask, tensor_mask=0):
        pairs = []
        for d in range(self.dp):
            for t in range(self.tensor):
                there = (d ^ dp_mask) * self.tensor + (t ^ tensor_mask)
                pairs.append((d * self.tensor + t, there))
        return lax.ppermute(v, AXES, pairs)

    def flip_y(self, v):
        return self.flip(v, 1)

    def flip_l(self, v):
        return self.flip(v, 2)

    def flip_x(self, v):
        return self.flip(v, 0, 2)

    def flip_c(self, v):
        return self.flip(v, 0, 1)

    def dp_sum(self, v):
        for bit in range(self.bits):
            v = v + self.flip(v, 1 << bit)
        return v

    def far_gather(self, v):
        pieces = [v]
        bit = 4
        while bit < self.dp:
            sent = pieces[0] if len(pieces) == 1 else jnp.stack(pieces)
            got = self.flip(sent, bit)
            pieces = pieces + ([got] if len(pieces) == 1 else [got[k] for k in range(len(pieces))])
            bit *= 2
        return pieces

    def absolute(self, pieces, axis):
        if self.far == 2:
            return in_order(self.f, *pieces, axis)
        stack = jnp.stack(pieces)
        return jnp.concatenate(
            [
                lax.dynamic_index_in_dim(stack, jnp.bitwise_xor(self.f, n), 0, keepdims=False)
                for n in range(self.far)
            ],
            axis=axis,
        )

    def far_reduce(self, pieces, *deps):
        bit = self.dp // 2
        while bit >= 4:
            n = len(pieces) // 2
            sent = pieces[n:]
            got = self.flip(sent[0] if n == 1 else jnp.stack(sent), bit)
            got = after(got, *deps) if deps else got
            got = [got] if n == 1 else [got[k] for k in range(n)]
            pieces = [
                p.astype(F32) + g.astype(F32) if n == 1 else (p.astype(F32) + g.astype(F32)).astype(BF)
                for p, g in zip(pieces[:n], got)
            ]
            bit //= 2
        return pieces[0]

    def cube_gather(self, v):
        parts = [v[a:b] for a, b in part_rows(v.shape[0])]
        for step in range(2):
            got = [self.cube_flip(n, step, part) for n, part in enumerate(parts)]
            parts = [jnp.concatenate(pair, axis=0) for pair in zip(parts, got)]
        last = [self.cube_flip(n, 2, part) for n, part in enumerate(parts)]
        return parts, last

    def cube_flip(self, part, step, v):
        orders = ((self.flip_l, self.flip_x, self.flip_y), (self.flip_y, self.flip_l, self.flip_x))
        return orders[part][step](v)

    def cube_reduce(self, near, last):
        got = [self.cube_flip(n, 2, v.astype(BF)) for n, v in enumerate(last)]
        parts = [a.astype(F32) + b.astype(F32) for a, b in zip(near, got)]
        for step in (1, 0):
            half = [v.shape[0] // 2 for v in parts]
            got = [
                self.cube_flip(n, step, v[h:].astype(BF)) for n, (v, h) in enumerate(zip(parts, half))
            ]
            parts = [v[:h] + g.astype(F32) for v, h, g in zip(parts, half, got)]
        return jnp.concatenate(parts, axis=0)


def part_rows(n):
    return [(0, n // 2), (n // 2, n)]


def split_parts(v, n):
    out, at = [], 0
    for a, b in part_rows(n):
        out.append(v[at : at + 4 * (b - a)])
        at += 4 * (b - a)
    return out


def in_order(flag, mine, other, axis):
    first = jnp.where(flag == 0, mine, other)
    second = jnp.where(flag == 0, other, mine)
    return jnp.concatenate([first, second], axis=axis)


def halves(flag, v, axis):
    n = v.shape[axis] // 2
    mine = lax.dynamic_slice_in_dim(v, flag * n, n, axis)
    other = lax.dynamic_slice_in_dim(v, (1 - flag) * n, n, axis)
    return mine, other


def after(value, *deps):
    return lax.optimization_barrier((value,) + deps)[0]


def pin(*values):
    return lax.optimization_barrier(values)


def nt(left, right):
    return lax.dot_general(left, right, (((1,), (1,)), ((), ())), preferred_element_type=F32)


def tn(left, right):
    return lax.dot_general(left, right, (((0,), (0,)), ((), ())), preferred_element_type=F32)


def dot(left, right):
    return jnp.dot(left, right, preferred_element_type=F32)


def spin(v, cos, sin):
    half = v.shape[-1] // 2
    a, b = v[:, :half], v[:, half:]
    return jnp.concatenate([a * cos - b * sin, b * cos + a * sin], axis=-1)


def attend_kernel(far, *refs):
    me, states, cos_ref, sin_ref, seg_col, seg_row, *weights = refs[:10]
    n1_ref, qr_ref, kr_ref, v_ref, p_ref, o_ref = refs[10:]
    seq, width = states.shape
    rp = width // (4 * far)
    fq, fk = qr_ref.shape[1], kr_ref.shape[1]
    tile = min(128, seq)
    scale = 1.0 / math.sqrt(HEAD_SIZE)
    d = me[0]

    @pl.loop(0, seq // tile)
    def _(number):
        rows = pl.ds(pl.multiple_of(number * tile, tile), tile)
        xf = states[rows, :].astype(F32)
        recip = lax.rsqrt(jnp.mean(xf * xf, axis=-1, keepdims=True) + EPS)
        total = None
        for j in range(2):
            for i in range(2):
                for k in range(far):
                    at = jnp.bitwise_xor(d, 4 * k + 2 * i + j)
                    if rp % 128 == 0:
                        block = states[rows, pl.ds(pl.multiple_of(at * rp, 128), rp)].astype(F32)
                    else:
                        first = pl.multiple_of((at // 2) * (2 * rp), 128)
                        block = states[rows, pl.ds(first, 2 * rp)].astype(F32)
                        block = jnp.where(at % 2 == 0, block[:, :rp], block[:, rp:])
                    w = weights[2 * j + i]
                    gain = w[k, rp : rp + EXTRA, :rp][:1].astype(F32)
                    normed = (block * recip * gain).astype(BF)
                    place = ((j * 2 + i) * far + k) * rp
                    n1_ref[rows, place : place + rp] = normed
                    part = dot(normed, w[k, :rp, :])
                    total = part if total is None else total + part
        cos, sin = cos_ref[rows, :], sin_ref[rows, :]
        for head in range(fq // HEAD_SIZE):
            block = slice(head * HEAD_SIZE, (head + 1) * HEAD_SIZE)
            qr_ref[rows, block] = spin(total[:, block], cos, sin).astype(BF)
        for head in range(fk // HEAD_SIZE):
            block = slice(head * HEAD_SIZE, (head + 1) * HEAD_SIZE)
            at = fq + head * HEAD_SIZE
            kr_ref[rows, block] = spin(total[:, at : at + HEAD_SIZE], cos, sin).astype(BF)
        v_ref[rows, :] = total[:, fq + fk :].astype(BF)

    rep = fq // fk
    for i in range(seq // tile):
        rows, keys = slice(i * tile, (i + 1) * tile), slice(0, (i + 1) * tile)
        shape = (tile, (i + 1) * tile)
        behind = lax.broadcasted_iota(jnp.int32, shape, 1) <= (
            lax.broadcasted_iota(jnp.int32, shape, 0) + i * tile
        )
        allowed = (seg_col[rows, :] == seg_row[:, keys]) & behind
        for head in range(fq // HEAD_SIZE):
            block = slice(head * HEAD_SIZE, (head + 1) * HEAD_SIZE)
            k = head // rep
            kblock = slice(k * HEAD_SIZE, (k + 1) * HEAD_SIZE)
            s = nt(qr_ref[rows, block], kr_ref[keys, kblock]) * scale
            s = jnp.where(allowed, s, -1e30)
            e = jnp.exp(s - jnp.max(s, axis=-1, keepdims=True))
            p = (e / jnp.sum(e, axis=-1, keepdims=True)).astype(BF)
            p_ref[head, rows, keys] = p
            o_ref[rows, block] = dot(p, v_ref[keys, kblock]).astype(BF)


def attend(me, states, cos, sin, segments, weights, fq, fk, far):
    seq, width = states.shape
    shapes = [
        jax.ShapeDtypeStruct((seq, width), BF),
        jax.ShapeDtypeStruct((seq, fq), BF),
        jax.ShapeDtypeStruct((seq, fk), BF),
        jax.ShapeDtypeStruct((seq, fk), BF),
        jax.ShapeDtypeStruct((fq // HEAD_SIZE, seq, seq), BF),
        jax.ShapeDtypeStruct((seq, fq), BF),
    ]
    vmem = pl.BlockSpec(memory_space=pltpu.VMEM)
    flops = 2 * seq * width * (fq + 2 * fk) + 4 * seq * seq * fq
    return pl.pallas_call(
        functools.partial(attend_kernel, far),
        out_shape=shapes,
        in_specs=[pl.BlockSpec(memory_space=pltpu.SMEM)] + [vmem] * 9,
        out_specs=[vmem] * 6,
        compiler_params=pltpu.CompilerParams(vmem_limit_bytes=LIMIT),
        cost_estimate=pl.CostEstimate(
            flops=flops, bytes_accessed=12 << 20, transcendentals=seq * seq * 2
        ),
        name="attend",
    )(me, states, cos, sin, segments[:, None], segments[None, :], *weights)


def attend_back_kernel(far, *refs):
    me, dh, w_o, qr_ref, kr_ref, v_ref, p_ref, cos_ref, sin_ref, *weights = refs[:13]
    d_ref, send_ref, keep_ref = refs[13:16]
    do_ref, dk_ref, dv_ref = refs[16:]
    seq, width = dh.shape
    rp = width // (4 * far)
    fq, fk = qr_ref.shape[1], kr_ref.shape[1]
    tile = min(128, seq)
    scale = 1.0 / math.sqrt(HEAD_SIZE)
    rep = fq // fk

    @pl.loop(0, seq // tile)
    def _(i):
        rows = pl.ds(pl.multiple_of(i * tile, tile), tile)
        do_ref[rows, :] = nt(dh[rows, :], w_o[...]).astype(BF)

    dk_ref[...] = jnp.zeros_like(dk_ref)
    dv_ref[...] = jnp.zeros_like(dv_ref)
    for i in range(seq // tile):
        rows, keys = slice(i * tile, (i + 1) * tile), slice(0, (i + 1) * tile)
        cos, sin = cos_ref[rows, :], -sin_ref[rows, :]
        for head in range(fq // HEAD_SIZE):
            block = slice(head * HEAD_SIZE, (head + 1) * HEAD_SIZE)
            k = head // rep
            kblock = slice(k * HEAD_SIZE, (k + 1) * HEAD_SIZE)
            do = do_ref[rows, block]
            pb = p_ref[head, rows, keys]
            p = pb.astype(F32)
            dp = nt(do, v_ref[keys, kblock])
            inner = jnp.sum(p * dp, axis=-1, keepdims=True)
            ds = (p * (dp - inner)).astype(BF)
            dq = dot(ds, kr_ref[keys, kblock]) * scale
            d_ref[rows, block] = spin(dq, cos, sin).astype(BF)
            dk_ref[keys, kblock] += tn(ds, qr_ref[rows, block])
            dv_ref[keys, kblock] += tn(pb, do)
    for head in range(fk // HEAD_SIZE):
        block = slice(head * HEAD_SIZE, (head + 1) * HEAD_SIZE)
        at = fq + head * HEAD_SIZE
        d_ref[:, at : at + HEAD_SIZE] = spin(
            dk_ref[:, block] * scale, cos_ref[...], -sin_ref[...]
        ).astype(BF)
    d_ref[:, fq + fk :] = dv_ref[...].astype(BF)

    tok = seq // 4
    mine, d = me[1], me[0]
    for side in range(2):
        out = slice(side * tok, (side + 1) * tok)
        for ref, which in ((send_ref, 1 - mine), (keep_ref, mine)):
            rows = pl.ds(pl.multiple_of((side * 2 + which) * tok, tok), tok)
            grad = d_ref[rows, :]
            for i in range(2):
                for k in range(far):
                    values = [
                        nt(grad, weights[2 * j + i][k, :rp, :]).astype(BF) for j in range(2)
                    ]
                    at = jnp.bitwise_xor(d, 4 * k + 2 * i)
                    if rp % 128 == 0:
                        for j in range(2):
                            place = pl.multiple_of(jnp.bitwise_xor(at, j) * rp, 128)
                            ref[out, pl.ds(place, rp)] = values[j]
                    else:
                        place = pl.multiple_of((at // 2) * (2 * rp), 128)
                        pair = [jnp.concatenate(v, axis=-1) for v in (values, values[::-1])]
                        ref[out, pl.ds(place, 2 * rp)] = jnp.where(at % 2 == 0, *pair)


def attend_back(me, dh, w_o, qr, kr, v, p, cos, sin, weights, far):
    seq, width = dh.shape
    fq, fk = qr.shape[1], kr.shape[1]
    vmem = pl.BlockSpec(memory_space=pltpu.VMEM)
    flops = 2 * seq * width * (fq + fq + 2 * fk) + 10 * seq * seq * fq
    return pl.pallas_call(
        functools.partial(attend_back_kernel, far),
        out_shape=[
            jax.ShapeDtypeStruct((seq, fq + 2 * fk), BF),
            jax.ShapeDtypeStruct((seq // 2, width), BF),
            jax.ShapeDtypeStruct((seq // 2, width), BF),
        ],
        in_specs=[pl.BlockSpec(memory_space=pltpu.SMEM)] + [vmem] * 12,
        out_specs=[vmem] * 3,
        scratch_shapes=[
            pltpu.VMEM((seq, fq), BF),
            pltpu.VMEM((seq, fk), F32),
            pltpu.VMEM((seq, fk), F32),
        ],
        compiler_params=pltpu.CompilerParams(vmem_limit_bytes=LIMIT),
        cost_estimate=pl.CostEstimate(flops=flops, bytes_accessed=16 << 20, transcendentals=0),
        name="attend_back",
    )(me, dh, w_o, qr, kr, v, p, cos, sin, *weights)


def tables(places, width):
    halfway = width // 2
    counter = jnp.arange(halfway, dtype=jnp.float32)
    inverse = jnp.exp(counter * (-2.0 * math.log(THETA) / width))
    angles = places.astype(jnp.float32)[..., None] * inverse
    return (jnp.cos(angles), jnp.sin(angles))


def rms_scale(value_rows):
    return lax.rsqrt(jnp.mean(value_rows * value_rows, axis=-1, keepdims=True) + EPS)


def norm_back(grad_normed, unit_rows, recip_rows, gain_full):
    scaled = grad_normed * gain_full
    gain_grad = jnp.sum(grad_normed * unit_rows, axis=0)
    grad_rows = recip_rows * (
        scaled - unit_rows * jnp.mean(scaled * unit_rows, axis=-1, keepdims=True)
    )
    return (gain_grad, grad_rows)


def per_device(
    states,
    teacher,
    segments,
    positions,
    w_q,
    key_matrix,
    value_matrix,
    w_o,
    w_gate,
    w_up,
    w_down,
    norm1_gain,
    norm2_gain,
):
    net = Net()
    far = net.far
    seq, width = states.shape
    rp = w_q.shape[0]
    tok = seq // 4
    fq, fk = w_q.shape[1], key_matrix.shape[1]
    fqkv = fq + 2 * fk
    sub = w_gate.shape[1] // 4

    def blocks_at(a, n, places, axis):
        return jnp.concatenate(
            [lax.dynamic_slice_in_dim(a, at * n, n, axis) for at in places], axis=axis
        )

    def add(a, b):
        return (a.astype(F32) + b.astype(F32)).astype(BF)

    live = (segments > 0).astype(F32)
    alive = jnp.sum(live)
    high = jnp.floor(alive / 256.0)
    low = alive - high * 256.0
    rider = jnp.concatenate([norm1_gain, norm2_gain, jnp.zeros((fqkv - 2 * rp,), BF)])
    rider = jnp.stack([rider, jnp.pad(jnp.stack([high, low]).astype(BF), (0, fqkv - 2))])
    rider = jnp.pad(rider, ((0, EXTRA - 2), (0, 0)))
    qkv = jnp.concatenate(
        [jnp.concatenate([w_q, key_matrix, value_matrix], axis=1), rider], axis=0
    )

    def exchange(w, split, concat):
        return lax.all_to_all(
            w, "dp", split, concat, axis_index_groups=net.near_groups, tiled=True
        )

    def gather(w, axis):
        return lax.all_gather(
            w, "dp", axis=axis, axis_index_groups=net.far_groups, tiled=True
        )

    w_gate, w_up, w_down = after((w_gate, w_up, w_down), qkv)
    o_pair = in_order(net.y, w_o, net.flip_y(w_o), 1)
    qkv_own = jnp.stack(net.far_gather(qkv))
    gate = exchange(w_gate, 1, 0)
    up = exchange(after(w_up, gate), 1, 0)
    down = exchange(after(w_down, up), 0, 1)
    gate = gather(gate, 0)
    qkv_l, qkv_y = net.flip_l(qkv_own), net.flip_y(qkv_own)
    o_far = net.far_gather(after(o_pair, qkv_own))
    o_far = net.absolute(o_far, 1)
    o_l = net.flip_l(o_far)
    qkv_ly, up = pin(net.flip_y(qkv_l), up)
    up = gather(up, 0)
    qkv_ly, gate = pin(qkv_ly, gate)
    qkv_all = (qkv_own, qkv_l, qkv_y, qkv_ly)

    me = jnp.stack([net.d, net.c]).astype(jnp.int32)
    cos_table, sin_table = tables(positions, HEAD_SIZE)
    normed, qr, kr, v, p, attended = attend(
        me, states, cos_table, sin_table, segments, qkv_all, fq, fk, far
    )
    o_l = after(o_l, attended)
    parts = []
    for n in range(far):
        block = slice(n * 2 * rp, (n + 1) * 2 * rp)
        parts.append(in_order(net.l, o_far[:, block], o_l[:, block], 1))
    full_o = jnp.concatenate(parts, axis=1)

    rider = [w[k, rp : rp + 2] for w in qkv_all for k in range(far)]
    count = sum(e[1, 0].astype(F32) * 256.0 + e[1, 1].astype(F32) for e in rider)

    def gains(at):
        def piece(j, i, k):
            return qkv_all[2 * j + i][k, rp, at : at + rp].astype(F32)

        parts = []
        for k in range(far):
            pairs = [in_order(net.y, piece(0, i, k), piece(1, i, k), 0) for i in range(2)]
            parts.append(in_order(net.l, *pairs, 0))
        return net.absolute(parts, 0)[None, :]

    gain_one, gain_two = gains(0), gains(rp)

    def rows_of_core(a, which):
        return blocks_at(a, tok, [which, 2 + which], 0)

    send = net.flip_c(dot(rows_of_core(attended, 1 - net.c), full_o).astype(BF))
    keep = dot(rows_of_core(attended, net.c), full_o)
    keep, send = halves(net.x, keep + send.astype(F32), 0)
    attn_sum = keep + net.flip_x(send.astype(BF)).astype(F32)

    first_token = (net.x * 2 + net.c) * tok
    my_inputs = lax.dynamic_slice_in_dim(states, first_token, tok, 0).astype(F32)
    my_teacher = lax.dynamic_slice_in_dim(teacher, first_token, tok, 0).astype(F32)
    my_live = lax.dynamic_slice_in_dim(live, first_token, tok, 0)

    attn_sum, down = pin(attn_sum, down)
    down = gather(down, 1)
    gate = after(gate, attn_sum)
    full_gate = jnp.concatenate([gate, net.flip_c(gate)], axis=1)
    hidden = my_inputs + attn_sum
    recip_two = rms_scale(hidden)
    unit_two = hidden * recip_two
    near, last = net.cube_gather((unit_two * gain_two).astype(BF))
    up = after(up, *near)
    full_up = jnp.concatenate([up, net.flip_c(up)], axis=1)
    n2_near, n2_last = jnp.concatenate(near, axis=0), jnp.concatenate(last, axis=0)

    def act(n2):
        gate, up = dot(n2, full_gate), dot(n2, full_up)
        sig = jax.nn.sigmoid(gate)
        silu = gate * sig
        by_gate = (up * sig * (1.0 + gate * (1.0 - sig))).astype(BF)
        return (silu * up).astype(BF), by_gate, silu.astype(BF)

    act_near, by_gate_near, by_up_near = act(n2_near)
    act_last, by_gate_last, by_up_last = act(after(n2_last, act_near))
    down = after(down, act_last)
    full_down = jnp.concatenate([down, net.flip_c(down)], axis=0)
    y_last = dot(act_last, full_down).astype(BF)
    y_near = dot(after(act_near, y_last), full_down)
    mlp_sum = net.cube_reduce(split_parts(y_near, tok), split_parts(y_last, tok))
    output = hidden + mlp_sum
    error = (output - my_teacher) * my_live[:, None]
    factor = net.dp * seq / count
    grad_out = error * factor
    squares = jnp.sum(error * error)

    def share_tokens(a):
        a = in_order(net.x, a, net.flip_x(a), 0)
        b = net.flip_c(a)
        return jnp.concatenate(
            [in_order(net.c, a[:tok], b[:tok], 0), in_order(net.c, a[tok:], b[tok:], 0)], axis=0
        )

    near, last = net.cube_gather(grad_out.astype(BF))
    dy_all = jnp.concatenate(near + last, axis=0)
    act_all = jnp.concatenate([act_near, act_last], axis=0)
    n2_all = jnp.concatenate([n2_near, n2_last], axis=0)

    def sum_back(total, axis):
        return lax.psum_scatter(
            total, "dp", scatter_dimension=axis, axis_index_groups=net.far_groups, tiled=True
        )

    down_other = tn(act_all[:, sub:], dy_all).astype(BF)
    down_mine = tn(act_all[:, :sub], dy_all).astype(BF)
    down_got = net.flip_c(down_other)
    grad_active = nt(after(dy_all, down_mine), full_down)
    dg_all = (grad_active * jnp.concatenate([by_gate_near, by_gate_last], axis=0)).astype(BF)
    du_all = (grad_active * jnp.concatenate([by_up_near, by_up_last], axis=0)).astype(BF)
    dg_all, du_all, down_sum = pin(dg_all, du_all, add(down_mine, down_got))
    down_sum = sum_back(down_sum, 1)
    dn_all = nt(
        jnp.concatenate([dg_all, du_all], axis=1), jnp.concatenate([full_gate, full_up], axis=1)
    )
    dn_near, dn_last = dn_all[: 4 * tok], dn_all[4 * tok :].astype(BF)
    n2_all, dg_late, du_late = after((n2_all, dg_all, du_all), dn_last)
    gate_other = tn(n2_all, dg_late[:, sub:]).astype(BF)
    gate_mine = tn(n2_all, dg_late[:, :sub]).astype(BF)
    gate_sum = sum_back(add(gate_mine, net.flip_c(gate_other)), 0)
    up_other = tn(n2_all, du_late[:, sub:]).astype(BF)
    up_mine = tn(n2_all, du_late[:, :sub]).astype(BF)
    up_sum = sum_back(add(up_mine, net.flip_c(up_other)), 0)

    back_two = net.cube_reduce(split_parts(dn_near, tok), split_parts(dn_last, tok))
    gain_two_grad, hidden_from_norm = norm_back(back_two, unit_two, recip_two, gain_two)
    grad_hidden = grad_out + hidden_from_norm
    grad_hidden_low = share_tokens(grad_hidden.astype(BF))
    out_states = share_tokens(after(output.astype(BF), grad_hidden_low))

    grad_qkv, send, keep = attend_back(
        me, grad_hidden_low, full_o, qr, kr, v, p, cos_table, sin_table, qkv_all, far
    )
    back_one = (keep.astype(F32) + net.flip_c(send).astype(F32)).astype(BF)
    back_got = net.flip_x(back_one)
    dh_low, att, n1, g_qkv = after((grad_hidden_low, attended, normed, grad_qkv), send)
    grad_wqkv = tn(n1, g_qkv).astype(BF)
    grad_wo = tn(att, dh_low).astype(BF)

    half, quarter = width // 2, width // 4
    gq, gkv = grad_wqkv[:, :fq], grad_wqkv[:, fq:]
    gkv = [gkv[n * quarter : (n + 1) * quarter] for n in range(4)]
    q_got = net.flip_y(gq[half:])
    kv_got = net.flip_l(jnp.concatenate([gkv[1], gkv[3]], axis=0))
    q_got, gate_sum = pin(q_got, gate_sum)
    q_got, kv_got, back_got = pin(q_got, kv_got, back_got)
    gq = add(gq[:half], q_got)
    gkv = add(jnp.concatenate([gkv[0], gkv[2]], axis=0), kv_got)
    q_got = net.flip_l(gq[quarter:])
    kv_got = net.flip_y(gkv[quarter:])
    q_got, kv_got, up_sum = pin(q_got, kv_got, up_sum)
    gqkv = jnp.concatenate([add(gq[:quarter], q_got), add(gkv[:quarter], kv_got)], axis=1)

    other = blocks_at(grad_wo, rp, [2 * n + 1 - net.y for n in range(2 * far)], 1)
    go = add(
        blocks_at(grad_wo, rp, [2 * n + net.y for n in range(2 * far)], 1), net.flip_y(other)
    )
    other = blocks_at(go, rp, [2 * n + 1 - net.l for n in range(far)], 1)
    go = add(blocks_at(go, rp, [2 * n + net.l for n in range(far)], 1), net.flip_l(other))

    def far_blocks(a):
        n = a.shape[0] // far
        return [a[k * n : (k + 1) * n] for k in range(far)]

    go = [
        lax.dynamic_slice_in_dim(go, jnp.bitwise_xor(net.f, k) * rp, rp, 1) for k in range(far)
    ]
    result_qkv = net.far_reduce(far_blocks(gqkv)).astype(F32)
    result_o = net.far_reduce(go).astype(F32)
    result_q = result_qkv[:, :fq]
    result_k, result_v = result_qkv[:, fq : fq + fk], result_qkv[:, fq + fk :]

    result_down = exchange(after(down_sum, send), 1, 0).astype(F32)
    result_gate = exchange(after(gate_sum, back_got), 0, 1).astype(F32)
    result_up = exchange(after(up_sum, far_blocks(gqkv)[0]), 0, 1).astype(F32)

    back_one = back_one.astype(F32) + back_got.astype(F32)
    xf = rows_of_core(states, net.c).astype(F32)
    recip_mine = rms_scale(xf)
    gain_one_grad, from_norm = norm_back(back_one, xf * recip_mine, recip_mine, gain_one)
    grad_input = rows_of_core(grad_hidden_low, net.c).astype(F32) + from_norm
    grad_other = net.flip_c(grad_input)
    grad_input = jnp.concatenate(
        [
            in_order(net.c, grad_input[:tok], grad_other[:tok], 0),
            in_order(net.c, grad_input[tok:], grad_other[tok:], 0),
        ],
        axis=0,
    )

    small = jnp.concatenate([0.5 * gain_one_grad, gain_two_grad, jnp.full((128,), squares, F32)])
    small = small.reshape(-1, 128)
    small = small + net.flip_c(small)
    small = small + net.flip_x(small)
    small = net.dp_sum(small).reshape(-1)
    result_g1 = lax.dynamic_slice_in_dim(small[:width], net.d * rp, rp)
    result_g2 = lax.dynamic_slice_in_dim(small[width : 2 * width], net.d * rp, rp)
    loss_value = small[2 * width] / (count * width)
    return (
        out_states,
        grad_input,
        loss_value,
        result_q,
        result_k,
        result_v,
        result_o,
        result_gate,
        result_up,
        result_down,
        result_g1,
        result_g2,
    )


def solution(mesh):
    in_specs = (
        P("dp", None),
        P("dp", None),
        P("dp"),
        P("dp"),
        P("dp", "tensor"),
        P("dp", "tensor"),
        P("dp", "tensor"),
        P("tensor", "dp"),
        P("dp", "tensor"),
        P("dp", "tensor"),
        P("tensor", "dp"),
        P("dp"),
        P("dp"),
    )
    out_specs = (
        P("dp", None),
        P("dp", None),
        P(),
        P("dp", "tensor"),
        P("dp", "tensor"),
        P("dp", "tensor"),
        P("tensor", "dp"),
        P("dp", "tensor"),
        P("dp", "tensor"),
        P("tensor", "dp"),
        P("dp"),
        P("dp"),
    )
    return jax.shard_map(
        per_device, mesh=mesh, in_specs=in_specs, out_specs=out_specs, check_vma=False
    )
```

```python
import functools
import math

import jax
import jax.numpy as jnp
from jax import lax
from jax.experimental import pallas as pl
from jax.experimental.pallas import tpu as pltpu
from jax.sharding import PartitionSpec as P

HEAD_SIZE = 256

EPS = 1e-06
THETA = 1000042.0
AXES = ("dp", "tensor")
BF = jnp.bfloat16
F32 = jnp.float32
EXTRA = 16
LIMIT = 56 * 1024 * 1024


class Net:
    def __init__(self):
        self.dp = lax.axis_size("dp")
        self.tensor = lax.axis_size("tensor")
        self.bits = self.dp.bit_length() - 1
        self.far = self.dp // 4
        self.d = lax.axis_index("dp")
        t = lax.axis_index("tensor")
        self.y, self.l, self.f = self.d % 2, (self.d // 2) % 2, self.d // 4
        self.x, self.c = t // 2, t % 2
        self.near_groups = [[4 * f + low for low in range(4)] for f in range(self.far)]
        self.far_groups = [[4 * f + low for f in range(self.far)] for low in range(4)]

    def flip(self, v, dp_mask, tensor_mask=0):
        pairs = []
        for d in range(self.dp):
            for t in range(self.tensor):
                there = (d ^ dp_mask) * self.tensor + (t ^ tensor_mask)
                pairs.append((d * self.tensor + t, there))
        return lax.ppermute(v, AXES, pairs)

    def flip_y(self, v):
        return self.flip(v, 1)

    def flip_l(self, v):
        return self.flip(v, 2)

    def flip_x(self, v):
        return self.flip(v, 0, 2)

    def flip_c(self, v):
        return self.flip(v, 0, 1)

    def dp_sum(self, v):
        for bit in range(self.bits):
            v = v + self.flip(v, 1 << bit)
        return v

    def far_gather(self, v):
        pieces = [v]
        bit = 4
        while bit < self.dp:
            sent = pieces[0] if len(pieces) == 1 else jnp.stack(pieces)
            got = self.flip(sent, bit)
            pieces = pieces + ([got] if len(pieces) == 1 else [got[k] for k in range(len(pieces))])
            bit *= 2
        return pieces

    def absolute(self, pieces, axis):
        if self.far == 2:
            return in_order(self.f, *pieces, axis)
        stack = jnp.stack(pieces)
        return jnp.concatenate(
            [
                lax.dynamic_index_in_dim(stack, jnp.bitwise_xor(self.f, n), 0, keepdims=False)
                for n in range(self.far)
            ],
            axis=axis,
        )

    def far_reduce(self, pieces, *deps):
        bit = self.dp // 2
        while bit >= 4:
            n = len(pieces) // 2
            sent = pieces[n:]
            got = self.flip(sent[0] if n == 1 else jnp.stack(sent), bit)
            got = after(got, *deps) if deps else got
            got = [got] if n == 1 else [got[k] for k in range(n)]
            pieces = [
                p.astype(F32) + g.astype(F32) if n == 1 else (p.astype(F32) + g.astype(F32)).astype(BF)
                for p, g in zip(pieces[:n], got)
            ]
            bit //= 2
        return pieces[0]

    def cube_gather(self, v):
        parts = [v[a:b] for a, b in part_rows(v.shape[0])]
        for step in range(2):
            got = [self.cube_flip(n, step, part) for n, part in enumerate(parts)]
            parts = [jnp.concatenate(pair, axis=0) for pair in zip(parts, got)]
        last = [self.cube_flip(n, 2, part) for n, part in enumerate(parts)]
        return parts, last

    def cube_flip(self, part, step, v):
        orders = ((self.flip_l, self.flip_x, self.flip_y), (self.flip_y, self.flip_l, self.flip_x))
        return orders[part][step](v)

    def cube_reduce(self, near, last):
        got = [self.cube_flip(n, 2, v.astype(BF)) for n, v in enumerate(last)]
        parts = [a.astype(F32) + b.astype(F32) for a, b in zip(near, got)]
        for step in (1, 0):
            half = [v.shape[0] // 2 for v in parts]
            got = [
                self.cube_flip(n, step, v[h:].astype(BF)) for n, (v, h) in enumerate(zip(parts, half))
            ]
            parts = [v[:h] + g.astype(F32) for v, h, g in zip(parts, half, got)]
        return jnp.concatenate(parts, axis=0)


def part_rows(n):
    return [(0, n // 2), (n // 2, n)]


def split_parts(v, n):
    out, at = [], 0
    for a, b in part_rows(n):
        out.append(v[at : at + 4 * (b - a)])
        at += 4 * (b - a)
    return out


def in_order(flag, mine, other, axis):
    first = jnp.where(flag == 0, mine, other)
    second = jnp.where(flag == 0, other, mine)
    return jnp.concatenate([first, second], axis=axis)


def halves(flag, v, axis):
    n = v.shape[axis] // 2
    mine = lax.dynamic_slice_in_dim(v, flag * n, n, axis)
    other = lax.dynamic_slice_in_dim(v, (1 - flag) * n, n, axis)
    return mine, other


def after(value, *deps):
    return lax.optimization_barrier((value,) + deps)[0]


def pin(*values):
    return lax.optimization_barrier(values)


def nt(left, right):
    return lax.dot_general(left, right, (((1,), (1,)), ((), ())), preferred_element_type=F32)


def tn(left, right):
    return lax.dot_general(left, right, (((0,), (0,)), ((), ())), preferred_element_type=F32)


def dot(left, right):
    return jnp.dot(left, right, preferred_element_type=F32)


def spin(v, cos, sin):
    half = v.shape[-1] // 2
    a, b = v[:, :half], v[:, half:]
    return jnp.concatenate([a * cos - b * sin, b * cos + a * sin], axis=-1)


def attend_kernel(far, *refs):
    me, states, cos_ref, sin_ref, seg_col, seg_row, *weights = refs[:10]
    n1_ref, qr_ref, kr_ref, v_ref, p_ref, o_ref = refs[10:]
    seq, width = states.shape
    rp = width // (4 * far)
    fq, fk = qr_ref.shape[1], kr_ref.shape[1]
    tile = min(128, seq)
    scale = 1.0 / math.sqrt(HEAD_SIZE)
    d = me[0]

    @pl.loop(0, seq // tile)
    def _(number):
        rows = pl.ds(pl.multiple_of(number * tile, tile), tile)
        xf = states[rows, :].astype(F32)
        recip = lax.rsqrt(jnp.mean(xf * xf, axis=-1, keepdims=True) + EPS)
        total = None
        for j in range(2):
            for i in range(2):
                for k in range(far):
                    at = jnp.bitwise_xor(d, 4 * k + 2 * i + j)
                    if rp % 128 == 0:
                        block = states[rows, pl.ds(pl.multiple_of(at * rp, 128), rp)].astype(F32)
                    else:
                        first = pl.multiple_of((at // 2) * (2 * rp), 128)
                        block = states[rows, pl.ds(first, 2 * rp)].astype(F32)
                        block = jnp.where(at % 2 == 0, block[:, :rp], block[:, rp:])
                    w = weights[2 * j + i]
                    gain = w[k, rp : rp + EXTRA, :rp][:1].astype(F32)
                    normed = (block * recip * gain).astype(BF)
                    place = ((j * 2 + i) * far + k) * rp
                    n1_ref[rows, place : place + rp] = normed
                    part = dot(normed, w[k, :rp, :])
                    total = part if total is None else total + part
        cos, sin = cos_ref[rows, :], sin_ref[rows, :]
        for head in range(fq // HEAD_SIZE):
            block = slice(head * HEAD_SIZE, (head + 1) * HEAD_SIZE)
            qr_ref[rows, block] = spin(total[:, block], cos, sin).astype(BF)
        for head in range(fk // HEAD_SIZE):
            block = slice(head * HEAD_SIZE, (head + 1) * HEAD_SIZE)
            at = fq + head * HEAD_SIZE
            kr_ref[rows, block] = spin(total[:, at : at + HEAD_SIZE], cos, sin).astype(BF)
        v_ref[rows, :] = total[:, fq + fk :].astype(BF)

    rep = fq // fk
    for i in range(seq // tile):
        rows, keys = slice(i * tile, (i + 1) * tile), slice(0, (i + 1) * tile)
        shape = (tile, (i + 1) * tile)
        behind = lax.broadcasted_iota(jnp.int32, shape, 1) <= (
            lax.broadcasted_iota(jnp.int32, shape, 0) + i * tile
        )
        allowed = (seg_col[rows, :] == seg_row[:, keys]) & behind
        for head in range(fq // HEAD_SIZE):
            block = slice(head * HEAD_SIZE, (head + 1) * HEAD_SIZE)
            k = head // rep
            kblock = slice(k * HEAD_SIZE, (k + 1) * HEAD_SIZE)
            s = nt(qr_ref[rows, block], kr_ref[keys, kblock]) * scale
            s = jnp.where(allowed, s, -1e30)
            e = jnp.exp(s - jnp.max(s, axis=-1, keepdims=True))
            p = (e / jnp.sum(e, axis=-1, keepdims=True)).astype(BF)
            p_ref[head, rows, keys] = p
            o_ref[rows, block] = dot(p, v_ref[keys, kblock]).astype(BF)


def attend(me, states, cos, sin, segments, weights, fq, fk, far):
    seq, width = states.shape
    shapes = [
        jax.ShapeDtypeStruct((seq, width), BF),
        jax.ShapeDtypeStruct((seq, fq), BF),
        jax.ShapeDtypeStruct((seq, fk), BF),
        jax.ShapeDtypeStruct((seq, fk), BF),
        jax.ShapeDtypeStruct((fq // HEAD_SIZE, seq, seq), BF),
        jax.ShapeDtypeStruct((seq, fq), BF),
    ]
    vmem = pl.BlockSpec(memory_space=pltpu.VMEM)
    flops = 2 * seq * width * (fq + 2 * fk) + 4 * seq * seq * fq
    return pl.pallas_call(
        functools.partial(attend_kernel, far),
        out_shape=shapes,
        in_specs=[pl.BlockSpec(memory_space=pltpu.SMEM)] + [vmem] * 9,
        out_specs=[vmem] * 6,
        compiler_params=pltpu.CompilerParams(vmem_limit_bytes=LIMIT),
        cost_estimate=pl.CostEstimate(
            flops=flops, bytes_accessed=12 << 20, transcendentals=seq * seq * 2
        ),
        name="attend",
    )(me, states, cos, sin, segments[:, None], segments[None, :], *weights)


def attend_back_kernel(far, *refs):
    me, dh, w_o, qr_ref, kr_ref, v_ref, p_ref, cos_ref, sin_ref, *weights = refs[:13]
    d_ref, send_ref, keep_ref = refs[13:16]
    do_ref, dk_ref, dv_ref = refs[16:]
    seq, width = dh.shape
    rp = width // (4 * far)
    fq, fk = qr_ref.shape[1], kr_ref.shape[1]
    tile = min(128, seq)
    scale = 1.0 / math.sqrt(HEAD_SIZE)
    rep = fq // fk

    @pl.loop(0, seq // tile)
    def _(i):
        rows = pl.ds(pl.multiple_of(i * tile, tile), tile)
        do_ref[rows, :] = nt(dh[rows, :], w_o[...]).astype(BF)

    dk_ref[...] = jnp.zeros_like(dk_ref)
    dv_ref[...] = jnp.zeros_like(dv_ref)
    for i in range(seq // tile):
        rows, keys = slice(i * tile, (i + 1) * tile), slice(0, (i + 1) * tile)
        cos, sin = cos_ref[rows, :], -sin_ref[rows, :]
        for head in range(fq // HEAD_SIZE):
            block = slice(head * HEAD_SIZE, (head + 1) * HEAD_SIZE)
            k = head // rep
            kblock = slice(k * HEAD_SIZE, (k + 1) * HEAD_SIZE)
            do = do_ref[rows, block]
            pb = p_ref[head, rows, keys]
            p = pb.astype(F32)
            dp = nt(do, v_ref[keys, kblock])
            inner = jnp.sum(p * dp, axis=-1, keepdims=True)
            ds = (p * (dp - inner)).astype(BF)
            dq = dot(ds, kr_ref[keys, kblock]) * scale
            d_ref[rows, block] = spin(dq, cos, sin).astype(BF)
            dk_ref[keys, kblock] += tn(ds, qr_ref[rows, block])
            dv_ref[keys, kblock] += tn(pb, do)
    for head in range(fk // HEAD_SIZE):
        block = slice(head * HEAD_SIZE, (head + 1) * HEAD_SIZE)
        at = fq + head * HEAD_SIZE
        d_ref[:, at : at + HEAD_SIZE] = spin(
            dk_ref[:, block] * scale, cos_ref[...], -sin_ref[...]
        ).astype(BF)
    d_ref[:, fq + fk :] = dv_ref[...].astype(BF)

    tok = seq // 4
    mine, d = me[1], me[0]
    for side in range(2):
        out = slice(side * tok, (side + 1) * tok)
        for ref, which in ((send_ref, 1 - mine), (keep_ref, mine)):
            rows = pl.ds(pl.multiple_of((side * 2 + which) * tok, tok), tok)
            grad = d_ref[rows, :]
            for i in range(2):
                for k in range(far):
                    values = [
                        nt(grad, weights[2 * j + i][k, :rp, :]).astype(BF) for j in range(2)
                    ]
                    at = jnp.bitwise_xor(d, 4 * k + 2 * i)
                    if rp % 128 == 0:
                        for j in range(2):
                            place = pl.multiple_of(jnp.bitwise_xor(at, j) * rp, 128)
                            ref[out, pl.ds(place, rp)] = values[j]
                    else:
                        place = pl.multiple_of((at // 2) * (2 * rp), 128)
                        pair = [jnp.concatenate(v, axis=-1) for v in (values, values[::-1])]
                        ref[out, pl.ds(place, 2 * rp)] = jnp.where(at % 2 == 0, *pair)


def attend_back(me, dh, w_o, qr, kr, v, p, cos, sin, weights, far):
    seq, width = dh.shape
    fq, fk = qr.shape[1], kr.shape[1]
    vmem = pl.BlockSpec(memory_space=pltpu.VMEM)
    flops = 2 * seq * width * (fq + fq + 2 * fk) + 10 * seq * seq * fq
    return pl.pallas_call(
        functools.partial(attend_back_kernel, far),
        out_shape=[
            jax.ShapeDtypeStruct((seq, fq + 2 * fk), BF),
            jax.ShapeDtypeStruct((seq // 2, width), BF),
            jax.ShapeDtypeStruct((seq // 2, width), BF),
        ],
        in_specs=[pl.BlockSpec(memory_space=pltpu.SMEM)] + [vmem] * 12,
        out_specs=[vmem] * 3,
        scratch_shapes=[
            pltpu.VMEM((seq, fq), BF),
            pltpu.VMEM((seq, fk), F32),
            pltpu.VMEM((seq, fk), F32),
        ],
        compiler_params=pltpu.CompilerParams(vmem_limit_bytes=LIMIT),
        cost_estimate=pl.CostEstimate(flops=flops, bytes_accessed=16 << 20, transcendentals=0),
        name="attend_back",
    )(me, dh, w_o, qr, kr, v, p, cos, sin, *weights)


def tables(places, width):
    halfway = width // 2
    counter = jnp.arange(halfway, dtype=jnp.float32)
    inverse = jnp.exp(counter * (-2.0 * math.log(THETA) / width))
    angles = places.astype(jnp.float32)[..., None] * inverse
    return (jnp.cos(angles), jnp.sin(angles))


def rms_scale(value_rows):
    return lax.rsqrt(jnp.mean(value_rows * value_rows, axis=-1, keepdims=True) + EPS)


def norm_back(grad_normed, unit_rows, recip_rows, gain_full):
    scaled = grad_normed * gain_full
    gain_grad = jnp.sum(grad_normed * unit_rows, axis=0)
    grad_rows = recip_rows * (
        scaled - unit_rows * jnp.mean(scaled * unit_rows, axis=-1, keepdims=True)
    )
    return (gain_grad, grad_rows)


def per_device(
    states,
    teacher,
    segments,
    positions,
    w_q,
    key_matrix,
    value_matrix,
    w_o,
    w_gate,
    w_up,
    w_down,
    norm1_gain,
    norm2_gain,
):
    net = Net()
    far = net.far
    seq, width = states.shape
    rp = w_q.shape[0]
    tok = seq // 4
    fq, fk = w_q.shape[1], key_matrix.shape[1]
    fqkv = fq + 2 * fk
    sub = w_gate.shape[1] // 4

    def blocks_at(a, n, places, axis):
        return jnp.concatenate(
            [lax.dynamic_slice_in_dim(a, at * n, n, axis) for at in places], axis=axis
        )

    def add(a, b):
        return (a.astype(F32) + b.astype(F32)).astype(BF)

    live = (segments > 0).astype(F32)
    alive = jnp.sum(live)
    high = jnp.floor(alive / 256.0)
    low = alive - high * 256.0
    rider = jnp.concatenate([norm1_gain, norm2_gain, jnp.zeros((fqkv - 2 * rp,), BF)])
    rider = jnp.stack([rider, jnp.pad(jnp.stack([high, low]).astype(BF), (0, fqkv - 2))])
    rider = jnp.pad(rider, ((0, EXTRA - 2), (0, 0)))
    qkv = jnp.concatenate(
        [jnp.concatenate([w_q, key_matrix, value_matrix], axis=1), rider], axis=0
    )

    def exchange(w, split, concat):
        return lax.all_to_all(
            w, "dp", split, concat, axis_index_groups=net.near_groups, tiled=True
        )

    def gather(w, axis):
        return lax.all_gather(
            w, "dp", axis=axis, axis_index_groups=net.far_groups, tiled=True
        )

    w_gate, w_up, w_down = after((w_gate, w_up, w_down), qkv)
    o_pair = in_order(net.y, w_o, net.flip_y(w_o), 1)
    qkv_own = jnp.stack(net.far_gather(qkv))
    gate = exchange(w_gate, 1, 0)
    up = exchange(after(w_up, gate), 1, 0)
    down = exchange(after(w_down, up), 0, 1)
    gate = gather(gate, 0)
    qkv_l, qkv_y = net.flip_l(qkv_own), net.flip_y(qkv_own)
    o_far = net.far_gather(after(o_pair, qkv_own))
    o_far = net.absolute(o_far, 1)
    o_l = net.flip_l(o_far)
    qkv_ly, up = pin(net.flip_y(qkv_l), up)
    up = gather(up, 0)
    qkv_all = (qkv_own, qkv_l, qkv_y, qkv_ly)

    me = jnp.stack([net.d, net.c]).astype(jnp.int32)
    cos_table, sin_table = tables(positions, HEAD_SIZE)
    normed, qr, kr, v, p, attended = attend(
        me, states, cos_table, sin_table, segments, qkv_all, fq, fk, far
    )
    o_l = after(o_l, attended)
    parts = []
    for n in range(far):
        block = slice(n * 2 * rp, (n + 1) * 2 * rp)
        parts.append(in_order(net.l, o_far[:, block], o_l[:, block], 1))
    full_o = jnp.concatenate(parts, axis=1)

    rider = [w[k, rp : rp + 2] for w in qkv_all for k in range(far)]
    count = sum(e[1, 0].astype(F32) * 256.0 + e[1, 1].astype(F32) for e in rider)

    def gains(at):
        def piece(j, i, k):
            return qkv_all[2 * j + i][k, rp, at : at + rp].astype(F32)

        parts = []
        for k in range(far):
            pairs = [in_order(net.y, piece(0, i, k), piece(1, i, k), 0) for i in range(2)]
            parts.append(in_order(net.l, *pairs, 0))
        return net.absolute(parts, 0)[None, :]

    gain_one, gain_two = gains(0), gains(rp)

    def rows_of_core(a, which):
        return blocks_at(a, tok, [which, 2 + which], 0)

    send = net.flip_c(dot(rows_of_core(attended, 1 - net.c), full_o).astype(BF))
    keep = dot(rows_of_core(attended, net.c), full_o)
    keep, send = halves(net.x, keep + send.astype(F32), 0)
    attn_sum = keep + net.flip_x(send.astype(BF)).astype(F32)

    first_token = (net.x * 2 + net.c) * tok
    my_inputs = lax.dynamic_slice_in_dim(states, first_token, tok, 0).astype(F32)
    my_teacher = lax.dynamic_slice_in_dim(teacher, first_token, tok, 0).astype(F32)
    my_live = lax.dynamic_slice_in_dim(live, first_token, tok, 0)

    attn_sum, down = pin(attn_sum, down)
    down = gather(down, 1)
    gate = after(gate, attn_sum)
    full_gate = jnp.concatenate([gate, net.flip_c(gate)], axis=1)
    hidden = my_inputs + attn_sum
    recip_two = rms_scale(hidden)
    unit_two = hidden * recip_two
    near, last = net.cube_gather((unit_two * gain_two).astype(BF))
    up = after(up, *near)
    full_up = jnp.concatenate([up, net.flip_c(up)], axis=1)
    n2_near, n2_last = jnp.concatenate(near, axis=0), jnp.concatenate(last, axis=0)

    def act(n2):
        gate, up = dot(n2, full_gate), dot(n2, full_up)
        sig = jax.nn.sigmoid(gate)
        silu = gate * sig
        by_gate = (up * sig * (1.0 + gate * (1.0 - sig))).astype(BF)
        return (silu * up).astype(BF), by_gate, silu.astype(BF)

    act_near, by_gate_near, by_up_near = act(n2_near)
    act_last, by_gate_last, by_up_last = act(after(n2_last, act_near))
    down = after(down, act_last)
    full_down = jnp.concatenate([down, net.flip_c(down)], axis=0)
    y_last = dot(act_last, full_down).astype(BF)
    y_near = dot(after(act_near, y_last), full_down).astype(BF)
    mlp_sum = net.cube_reduce(split_parts(y_near, tok), split_parts(y_last, tok))
    output = hidden + mlp_sum
    error = (output - my_teacher) * my_live[:, None]
    factor = net.dp * seq / count
    grad_out = error * factor
    squares = jnp.sum(error * error)

    def share_tokens(a):
        a = in_order(net.x, a, net.flip_x(a), 0)
        b = net.flip_c(a)
        return jnp.concatenate(
            [in_order(net.c, a[:tok], b[:tok], 0), in_order(net.c, a[tok:], b[tok:], 0)], axis=0
        )

    near, last = net.cube_gather(grad_out.astype(BF))
    dy_all = jnp.concatenate(near + last, axis=0)
    act_all = jnp.concatenate([act_near, act_last], axis=0)
    n2_all = jnp.concatenate([n2_near, n2_last], axis=0)

    def sum_back(total, axis):
        return lax.psum_scatter(
            total, "dp", scatter_dimension=axis, axis_index_groups=net.far_groups, tiled=True
        )

    down_other = tn(act_all[:, sub:], dy_all).astype(BF)
    down_mine = tn(act_all[:, :sub], dy_all).astype(BF)
    down_got = net.flip_c(down_other)
    grad_active = nt(after(dy_all, down_mine), full_down)
    dg_all = (grad_active * jnp.concatenate([by_gate_near, by_gate_last], axis=0)).astype(BF)
    du_all = (grad_active * jnp.concatenate([by_up_near, by_up_last], axis=0)).astype(BF)
    dg_all, du_all, down_sum = pin(dg_all, du_all, add(down_mine, down_got))
    down_sum = sum_back(down_sum, 1)
    dn_all = nt(
        jnp.concatenate([dg_all, du_all], axis=1), jnp.concatenate([full_gate, full_up], axis=1)
    )
    dn_all = dn_all.astype(BF)
    dn_near, dn_last = dn_all[: 4 * tok], dn_all[4 * tok :]
    n2_all, dg_late, du_late = after((n2_all, dg_all, du_all), dn_last)
    gate_other = tn(n2_all, dg_late[:, sub:]).astype(BF)
    gate_mine = tn(n2_all, dg_late[:, :sub]).astype(BF)
    gate_sum = sum_back(add(gate_mine, net.flip_c(gate_other)), 0)
    up_other = tn(n2_all, du_late[:, sub:]).astype(BF)
    up_mine = tn(n2_all, du_late[:, :sub]).astype(BF)
    up_sum = sum_back(add(up_mine, net.flip_c(up_other)), 0)

    back_two = net.cube_reduce(split_parts(dn_near, tok), split_parts(dn_last, tok))
    gain_two_grad, hidden_from_norm = norm_back(back_two, unit_two, recip_two, gain_two)
    grad_hidden = grad_out + hidden_from_norm
    grad_hidden_low = share_tokens(grad_hidden.astype(BF))
    out_states = share_tokens(after(output.astype(BF), grad_hidden_low))

    grad_qkv, send, keep = attend_back(
        me, grad_hidden_low, full_o, qr, kr, v, p, cos_table, sin_table, qkv_all, far
    )
    back_one = (keep.astype(F32) + net.flip_c(send).astype(F32)).astype(BF)
    back_got = net.flip_x(back_one)
    dh_low, att, n1, g_qkv = after((grad_hidden_low, attended, normed, grad_qkv), send)
    grad_wqkv = tn(n1, g_qkv).astype(BF)
    grad_wo = tn(att, dh_low).astype(BF)

    half, quarter = width // 2, width // 4
    gq, gkv = grad_wqkv[:, :fq], grad_wqkv[:, fq:]
    gkv = [gkv[n * quarter : (n + 1) * quarter] for n in range(4)]
    q_got = net.flip_y(gq[half:])
    kv_got = net.flip_l(jnp.concatenate([gkv[1], gkv[3]], axis=0))
    q_got, gate_sum = pin(q_got, gate_sum)
    q_got, kv_got, back_got = pin(q_got, kv_got, back_got)
    gq = add(gq[:half], q_got)
    gkv = add(jnp.concatenate([gkv[0], gkv[2]], axis=0), kv_got)
    q_got = net.flip_l(gq[quarter:])
    kv_got = net.flip_y(gkv[quarter:])
    q_got, kv_got, up_sum = pin(q_got, kv_got, up_sum)
    gqkv = jnp.concatenate([add(gq[:quarter], q_got), add(gkv[:quarter], kv_got)], axis=1)

    other = blocks_at(grad_wo, rp, [2 * n + 1 - net.y for n in range(2 * far)], 1)
    go = add(
        blocks_at(grad_wo, rp, [2 * n + net.y for n in range(2 * far)], 1), net.flip_y(other)
    )
    other = blocks_at(go, rp, [2 * n + 1 - net.l for n in range(far)], 1)
    go = add(blocks_at(go, rp, [2 * n + net.l for n in range(far)], 1), net.flip_l(other))

    def far_blocks(a):
        n = a.shape[0] // far
        return [a[k * n : (k + 1) * n] for k in range(far)]

    go = [
        lax.dynamic_slice_in_dim(go, jnp.bitwise_xor(net.f, k) * rp, rp, 1) for k in range(far)
    ]
    result_qkv = net.far_reduce(far_blocks(gqkv)).astype(F32)
    result_o = net.far_reduce(go).astype(F32)
    result_q = result_qkv[:, :fq]
    result_k, result_v = result_qkv[:, fq : fq + fk], result_qkv[:, fq + fk :]

    result_down = exchange(after(down_sum, send), 1, 0).astype(F32)
    result_gate = exchange(after(gate_sum, back_got), 0, 1).astype(F32)
    result_up = exchange(after(up_sum, far_blocks(gqkv)[0]), 0, 1).astype(F32)

    back_one = back_one.astype(F32) + back_got.astype(F32)
    xf = rows_of_core(states, net.c).astype(F32)
    recip_mine = rms_scale(xf)
    gain_one_grad, from_norm = norm_back(back_one, xf * recip_mine, recip_mine, gain_one)
    grad_input = rows_of_core(grad_hidden_low, net.c).astype(F32) + from_norm
    grad_other = net.flip_c(grad_input)
    grad_input = jnp.concatenate(
        [
            in_order(net.c, grad_input[:tok], grad_other[:tok], 0),
            in_order(net.c, grad_input[tok:], grad_other[tok:], 0),
        ],
        axis=0,
    )

    small = jnp.concatenate([0.5 * gain_one_grad, gain_two_grad, jnp.full((128,), squares, F32)])
    small = small.reshape(-1, 128)
    small = small + net.flip_c(small)
    small = small + net.flip_x(small)
    small = net.dp_sum(small).reshape(-1)
    result_g1 = lax.dynamic_slice_in_dim(small[:width], net.d * rp, rp)
    result_g2 = lax.dynamic_slice_in_dim(small[width : 2 * width], net.d * rp, rp)
    loss_value = small[2 * width] / (count * width)
    return (
        out_states,
        grad_input,
        loss_value,
        result_q,
        result_k,
        result_v,
        result_o,
        result_gate,
        result_up,
        result_down,
        result_g1,
        result_g2,
    )


def solution(mesh):
    in_specs = (
        P("dp", None),
        P("dp", None),
        P("dp"),
        P("dp"),
        P("dp", "tensor"),
        P("dp", "tensor"),
        P("dp", "tensor"),
        P("tensor", "dp"),
        P("dp", "tensor"),
        P("dp", "tensor"),
        P("tensor", "dp"),
        P("dp"),
        P("dp"),
    )
    out_specs = (
        P("dp", None),
        P("dp", None),
        P(),
        P("dp", "tensor"),
        P("dp", "tensor"),
        P("dp", "tensor"),
        P("tensor", "dp"),
        P("dp", "tensor"),
        P("dp", "tensor"),
        P("tensor", "dp"),
        P("dp"),
        P("dp"),
    )
    return jax.shard_map(
        per_device, mesh=mesh, in_specs=in_specs, out_specs=out_specs, check_vma=False
    )
```
